256 devices in a mesh: seq: 64 (over z_lo, x, y), fold: 4 (over z_hi, core).
Axes of the slice: x: 4, y: 4, z: 8 (z_hi: 2, z_lo: 4; z = z_hi * 4 + z_lo), core: 2. Of those that a mesh axis runs over, the one named last changes fastest.
Arguments:
- query: bfloat16 [65536, 1024], P(('seq', 'fold')), may hold values from -6 to 6
- keys: bfloat16 [65536, 128], P(('seq', 'fold')), may hold values from -6 to 6
- values: bfloat16 [65536, 128], P(('seq', 'fold')), may hold values from -6 to 6
- grad_out: bfloat16 [65536, 1024], P(('seq', 'fold')), may hold values from -6 to 6
- head_bias: float32 [8], replicated, may hold values from -7 to -4
- doc_ids: int32 [65536], P(('seq', 'fold')), may hold values from 0 to 255, never falling along the last dimension, each value on 1 to 2048 neighbouring positions
Outputs:
- grad_query: bfloat16 [65536, 1024], P(('seq', 'fold'))
- grad_keys: bfloat16 [65536, 128], P(('seq', 'fold'))
- grad_values: bfloat16 [65536, 128], P(('seq', 'fold'))
The draws below stay inside these ranges and needn't reach their ends.
Inputs may be any that keep to these rules, and one draw needn't show every extreme that they name: `doc_ids`: ids never fall along the sequence; every document has 1 to 2048 tokens, and one has exactly 2048.
All inputs are finite; a program needn't handle non-finite values.
Results may differ from the reference program's by a relative error of at most 0.005.
Values may be sent and summed in bfloat16 or wider, within the bound.
A program may use at most 128 MiB of HBM per device.

```python
import math
import jax
import jax.numpy as jnp
import numpy as np
from jax import lax

HEADS = 8
DH = 128
TOK_DEV = 256
MAXDOC = 2048
TOKENS = 65536
DOCS = 256


def block_scale(stream_key, shape, cuts, least, high):
    loudness = 1.0
    for axis_at, blocks in cuts:
        draws = jax.random.uniform(jax.random.fold_in(jax.random.fold_in(stream_key, 6), axis_at), (blocks,), jnp.float32, least / len(cuts), high / len(cuts))
        loudness = loudness * jnp.repeat(jnp.exp(draws), shape[axis_at] // blocks).reshape((-1,) + (1,) * (len(shape) - 1 - axis_at))
    return loudness


def split_up(amount, total, limit, lean):
    loads = [(1 << 20) // math.isqrt(grade ** lean) + 1 for grade in range(2, amount + 1)]
    surplus, holding = total - limit - (amount - 1), [1] * (amount - 1)
    while surplus > 0:
        movable = [i for i in range(amount - 1) if holding[i] < limit]
        pool, remaining = sum([loads[i] for i in movable]), surplus
        for i in movable:
            extra = min(limit - holding[i], max(1, remaining * loads[i] // pool), surplus)
            holding[i] = holding[i] + extra
            surplus = surplus - extra
    return np.array([limit] + holding)


def ragged_sizes(key, count, total, bound, lean):
    if count == 2:
        one = jax.random.randint(key, (), max(1, total - bound), min(bound, total - 1) + 1)
        return jnp.stack([one, total - one])
    lengths = jnp.asarray(split_up(count, total, bound, lean), jnp.int32)
    pairs = (count - 1) // 2
    donor, receiver = lengths[1:1 + 2 * pairs:2], lengths[2:2 + 2 * pairs:2]
    margin = jnp.minimum(donor - 1, bound - receiver)
    moved = jax.random.randint(jax.random.fold_in(key, 1), (pairs,), 0, 1 << 20) % (margin + 1)
    lengths = lengths.at[1:1 + 2 * pairs:2].set(donor - moved).at[2:2 + 2 * pairs:2].set(receiver + moved)
    return lengths[jax.random.permutation(jax.random.fold_in(key, 2), count)]


def noise(rng, dims, deviation, limit, shards=(), kind=jnp.bfloat16):
    values = jax.random.normal(rng, dims, jnp.float32) * deviation
    if len(shards) > 0:
        values = block_scale(rng, dims, shards, -0.22, 0.18) * values
    return jnp.clip(values, min=-limit, max=limit).astype(kind)


def setup_inputs(seed: int = 0) -> dict:
    arg_keys = jax.random.split(jax.random.key(seed), 7)
    query = noise(arg_keys[0], (TOKENS, HEADS * DH), 1.0, 6.0, ((0, 256),))
    keys = noise(arg_keys[1], (TOKENS, DH), 1.0, 6.0, ((0, 256),))
    values = noise(arg_keys[2], (TOKENS, DH), 1.0, 6.0, ((0, 256),))
    grad_out = noise(arg_keys[3], (TOKENS, HEADS * DH), 1.0, 6.0, ((0, 256),))
    head_bias = jnp.clip(jax.random.uniform(arg_keys[4], (HEADS,), jnp.float32, -7.0, -4.0), -7.0, -4.0)
    doc_ids = jnp.searchsorted(jnp.cumsum(ragged_sizes(arg_keys[5], DOCS, TOKENS, MAXDOC, 2)), jnp.arange(TOKENS), side="right").astype(jnp.int32)
    return dict(query=query, keys=keys, values=values, grad_out=grad_out, head_bias=head_bias, doc_ids=doc_ids)


def block_grads(query_heads, grad_heads, key_block, value_block, weight_mask, head_bias):
    factor = 1.0 / math.sqrt(key_block.shape[1])
    heads = query_heads.shape[1]
    key_trans = key_block.T
    value_trans = value_block.T
    grad_value = jnp.zeros(key_block.shape, jnp.float32)
    grad_key = jnp.zeros(key_block.shape, jnp.float32)
    query_list = []
    for head in range(heads):
        query_one = query_heads[:, head, :]
        grad_one = grad_heads[:, head, :]
        scores = jnp.dot(query_one, key_trans, preferred_element_type=jnp.float32) * factor + head_bias[head]
        probs = jax.nn.sigmoid(scores) * weight_mask
        probs_low = probs.astype(jnp.bfloat16)
        grad_value = grad_value + jnp.dot(probs_low.T, grad_one, preferred_element_type=jnp.float32)
        grad_probs = jnp.dot(grad_one, value_trans, preferred_element_type=jnp.float32)
        grad_scores = (grad_probs * probs * (1.0 - probs)).astype(jnp.bfloat16)
        query_list.append(jnp.dot(grad_scores, key_block, preferred_element_type=jnp.float32) * factor)
        grad_key = grad_key + jnp.dot(grad_scores.T, query_one, preferred_element_type=jnp.float32) * factor
    grad_query = jnp.stack(query_list, axis=1)
    return (grad_query, grad_key, grad_value)

def reference(query, keys, values, grad_out, head_bias, doc_ids):
    tokens, head_dim = keys.shape
    heads = query.shape[1] // head_dim
    rows = TOK_DEV
    reach = MAXDOC // rows
    blocks = tokens // rows
    front = reach * rows
    width = front + rows
    keys_pad = jnp.concatenate([jnp.zeros((front, head_dim), keys.dtype), keys])
    values_pad = jnp.concatenate([jnp.zeros((front, head_dim), values.dtype), values])
    ids_pad = jnp.concatenate([jnp.full((front,), -1, jnp.int32), doc_ids.astype(jnp.int32)])
    query_blocks = query.reshape(blocks, rows, heads, head_dim)
    grad_blocks = grad_out.reshape(blocks, rows, heads, head_dim)
    bias = head_bias.astype(jnp.float32)

    def step(carry, inputs):
        key_acc, value_acc = carry
        index, query_heads, grad_heads = inputs
        start = (index * rows).astype(jnp.int32)
        key_window = lax.dynamic_slice_in_dim(keys_pad, start, width, 0)
        value_window = lax.dynamic_slice_in_dim(values_pad, start, width, 0)
        id_window = lax.dynamic_slice_in_dim(ids_pad, start, width, 0)
        own_ids = lax.dynamic_slice_in_dim(ids_pad, start + front, rows, 0)
        key_pos = start - front + jnp.arange(width, dtype=jnp.int32)
        query_pos = start + jnp.arange(rows, dtype=jnp.int32)
        weight_mask = ((own_ids[:, None] == id_window[None, :]) & (key_pos[None, :] <= query_pos[:, None])).astype(jnp.float32)
        part_query, part_key, part_value = block_grads(query_heads, grad_heads, key_window, value_window, weight_mask, bias)
        key_acc = lax.dynamic_update_slice_in_dim(key_acc, lax.dynamic_slice_in_dim(key_acc, start, width, 0) + part_key, start, 0)
        value_acc = lax.dynamic_update_slice_in_dim(value_acc, lax.dynamic_slice_in_dim(value_acc, start, width, 0) + part_value, start, 0)
        return ((key_acc, value_acc), part_query)
    empty = jnp.zeros((front + tokens, head_dim), jnp.float32)
    (key_acc, value_acc), query_parts = lax.scan(step, (empty, empty), (jnp.arange(blocks, dtype=jnp.int32), query_blocks, grad_blocks))
    grad_query = query_parts.reshape(tokens, heads * head_dim).astype(jnp.bfloat16)
    return (grad_query, key_acc[front:].astype(jnp.bfloat16), value_acc[front:].astype(jnp.bfloat16))
```

```python
import functools
import math

import jax
import jax.numpy as jnp
from jax import lax
from jax.experimental import pallas as pl
from jax.experimental.pallas import tpu as pltpu
from jax.sharding import PartitionSpec as P

MAXDOC = 2048
MESH = pl.DeviceIdType.MESH
LOG2E = math.log2(math.e)
F32 = jnp.float32
BF16 = jnp.bfloat16


def dot_nt(a, b):
    return lax.dot_general(a, b, (((1,), (1,)), ((), ())), preferred_element_type=F32)


def dot_nn(a, b):
    return jnp.dot(a, b, preferred_element_type=F32)


def kernel(
    seq, fold, rows, dh, heads,
    bias_ref, ids_ref, query_ref, keys_ref, values_ref, grad_ref,
    out_query_ref, out_key_ref, out_value_ref,
    q_nat, q_tra, do_nat, do_tra, dom_nat, dom_tra, kv_own,
    blocks, sib_blocks, acc, own_part, part_d, part_o, sib_part, ret_out, ret_in,
    load_sem, fwd_send, fwd_recv, sib_send, sib_recv, sibp_send, sibp_recv, ret_send, ret_recv,
):
    peers = seq * fold
    me = lax.axis_index("seq") * fold + lax.axis_index("fold")
    odd = lax.rem(me, 2)
    hops = MAXDOC // rows // 2
    factor = 1.0 / math.sqrt(dh)

    def device(index):
        index = lax.rem(index + peers, peers)
        return (index // fold, lax.rem(index, fold))

    sibling = device(me + 1 - 2 * odd)

    barrier = pltpu.get_barrier_semaphore()
    for hop in range(1, hops + 1):
        for sign in (1, -1):
            pl.semaphore_signal(
                barrier, inc=1, device_id=device(me + sign * 2 * hop), device_id_type=MESH
            )
    pl.semaphore_signal(barrier, inc=1, device_id=sibling, device_id_type=MESH)

    cols = [pl.ds(h * dh, dh) for h in range(heads)]
    loads = [
        pltpu.make_async_copy(keys_ref, kv_own.at[0], load_sem.at[0]),
        pltpu.make_async_copy(values_ref, kv_own.at[1], load_sem.at[1]),
        pltpu.make_async_copy(query_ref, q_nat, load_sem.at[2]),
        pltpu.make_async_copy(grad_ref, do_nat, load_sem.at[3]),
    ]
    for load in loads:
        load.start()

    ids_row = ids_ref[...].astype(F32).reshape(1, rows)
    first = ids_row[:, 0:1]
    last = ids_row[:, rows - 1 : rows]
    ids_u = jnp.broadcast_to(ids_row, (rows, rows))
    ids_t = ids_u.T
    col_first = (ids_t[:, :dh] == first).astype(BF16)
    col_last = (ids_t[:, :dh] == last).astype(BF16)
    row_first = (ids_row == first).astype(BF16)
    row_last = (ids_row == last).astype(F32)

    def fwd(m):
        return pltpu.make_async_remote_copy(
            blocks.at[0], blocks.at[m], fwd_send.at[m - 1], fwd_recv.at[m - 1],
            device_id=device(me + 2 * m), device_id_type=MESH,
        )

    def to_sib(m):
        slot = m - odd
        return pltpu.make_async_remote_copy(
            blocks.at[m], sib_blocks.at[slot], sib_send.at[slot], sib_recv.at[slot],
            device_id=sibling, device_id_type=MESH,
        )

    def part_to_sib(slot):
        return pltpu.make_async_remote_copy(
            part_o.at[slot], sib_part.at[slot], sibp_send.at[slot], sibp_recv.at[slot],
            device_id=sibling, device_id_type=MESH,
        )

    def ret(m):
        return pltpu.make_async_remote_copy(
            ret_out.at[m - 1], ret_in.at[m - 1], ret_send.at[m - 1], ret_recv.at[m - 1],
            device_id=device(me - 2 * m), device_id_type=MESH,
        )

    loads[0].wait()
    loads[1].wait()
    blocks[0, pl.ds(0, rows)] = kv_own[0]
    blocks[0, pl.ds(rows, rows)] = kv_own[1] * col_last
    blocks[0, pl.ds(2 * rows, 16)] = jnp.broadcast_to(last, (16, dh)).astype(BF16)

    pl.semaphore_wait(barrier, 4 * hops // 2 + 1)
    for m in (2, 1, 4, 3):
        fwd(m).start()

    @pl.when(odd == 0)
    def _():
        to_sib(0).start()

    loads[2].wait()
    loads[3].wait()
    for h in range(heads):
        q_tra[cols[h], :] = q_nat[:, cols[h]].T
        do_tra[cols[h], :] = do_nat[:, cols[h]].T
    for h in range(heads):
        dom_nat[:, cols[h]] = do_nat[:, cols[h]] * col_first
        dom_tra[cols[h], :] = do_tra[cols[h], :] * row_first

    def block(k, v, g_nat, g_tra, mask, fresh):
        def scores(h):
            return dot_nt(q_nat[:, cols[h]], k), dot_nt(g_nat[:, cols[h]], v)

        grad_k = jnp.zeros((dh, rows), F32)
        grad_v = jnp.zeros((dh, rows), F32)
        ahead = scores(0)
        for h in range(heads):
            s, dp = ahead
            if h + 1 < heads:
                ahead = scores(h + 1)
            grow = jnp.exp2(s * (-factor * LOG2E) + bias_ref[h] * (-LOG2E))
            p = 1.0 / (1.0 + grow)
            if mask is not None:
                p = p * mask
            ds = (dp * (p * (1.0 - p))).astype(BF16)
            p = p.astype(BF16)
            if fresh:
                acc[:, cols[h]] = dot_nn(ds, k)
            else:
                acc[:, cols[h]] += dot_nn(ds, k)
            grad_v = grad_v + dot_nn(g_tra[cols[h], :], p)
            grad_k = grad_k + dot_nn(q_tra[cols[h], :], ds)
        return grad_k, grad_v

    iota_t = lax.broadcasted_iota(jnp.int32, (rows, rows), 0)
    iota_u = lax.broadcasted_iota(jnp.int32, (rows, rows), 1)
    mask = ((ids_t == ids_u) & (iota_u <= iota_t)).astype(F32)
    grad_k, grad_v = block(kv_own[0], kv_own[1], do_nat, do_tra, mask, True)
    own_part[pl.ds(0, dh)] = grad_k
    own_part[pl.ds(dh, dh)] = grad_v

    def arrived(m):
        fwd(m).wait_recv()

        @pl.when(m - odd < hops)
        def _():
            to_sib(m).start()

    def far_block(ref, part):
        gate = (ref[pl.ds(2 * rows, 16)][0:1].astype(F32) == first).astype(F32)
        k = ref[pl.ds(0, rows)]
        v = ref[pl.ds(rows, rows)] * gate.astype(BF16)
        grad_k, grad_v = block(k, v, dom_nat, dom_tra, None, False)
        part[pl.ds(0, dh)] = grad_k
        part[pl.ds(dh, dh)] = grad_v * jnp.concatenate([gate] * (rows // dh), axis=1)

    def order(step):
        return 2 * step + 2 - 5 * (step // 2)

    arrived(order(0))

    def body(step, carry):
        m = order(step)
        slot = lax.rem(m - 1 + odd, hops)
        to_sib(slot + odd).wait_recv()
        far_block(sib_blocks.at[slot], part_o.at[slot])
        part_to_sib(slot).start()

        @pl.when(step + 1 < hops)
        def _():
            arrived(order(step + 1))

        far_block(blocks.at[m], part_d)
        back = m - odd

        @pl.when(back < hops)
        def _():
            part_to_sib(back).wait_recv()
            ret_out[m - 1] = (part_d[...] + sib_part[back]).astype(BF16)

        @pl.when(back >= hops)
        def _():
            ret_out[m - 1] = part_d[...].astype(BF16)

        ret(m).start()
        return carry

    lax.fori_loop(0, hops, body, 0)

    out_query_ref[...] = (acc[...] * factor).astype(BF16)

    @pl.when(odd == 0)
    def _():
        part_to_sib(0).wait_recv()
        own_part[...] = own_part[...] + sib_part[0] * row_last

    total = own_part[...]
    for m in range(1, hops + 1):
        ret(m).wait_recv()
        total = total + ret_in[m - 1].astype(F32) * row_last
    out_key_ref[...] = (total[:dh] * factor).T.astype(BF16)
    out_value_ref[...] = total[dh:].T.astype(BF16)

    for m in range(1, hops + 1):
        fwd(m).wait_send()
        ret(m).wait_send()
        part_to_sib(m - 1).wait_send()
    for slot in range(hops):
        to_sib(slot + odd).wait_send()


def solution(mesh):
    seq, fold = mesh.shape["seq"], mesh.shape["fold"]

    def body(query, keys, values, grad_out, head_bias, doc_ids):
        rows, dh = keys.shape
        heads = query.shape[1] // dh
        hops = MAXDOC // rows // 2
        wide = heads * dh
        block = 2 * rows + 16
        vmem = pl.BlockSpec(memory_space=pltpu.VMEM)
        hbm = pl.BlockSpec(memory_space=pl.ANY)
        dma = pltpu.SemaphoreType.DMA
        return pl.pallas_call(
            functools.partial(kernel, seq, fold, rows, dh, heads),
            out_shape=(
                jax.ShapeDtypeStruct((rows, wide), BF16),
                jax.ShapeDtypeStruct((rows, dh), BF16),
                jax.ShapeDtypeStruct((rows, dh), BF16),
            ),
            in_specs=[pl.BlockSpec(memory_space=pltpu.SMEM), vmem, hbm, hbm, hbm, hbm],
            out_specs=(vmem, vmem, vmem),
            scratch_shapes=[
                pltpu.VMEM((rows, wide), BF16),
                pltpu.VMEM((wide, rows), BF16),
                pltpu.VMEM((rows, wide), BF16),
                pltpu.VMEM((wide, rows), BF16),
                pltpu.VMEM((rows, wide), BF16),
                pltpu.VMEM((wide, rows), BF16),
                pltpu.VMEM((2, rows, dh), BF16),
                pltpu.VMEM((hops + 1, block, dh), BF16),
                pltpu.VMEM((hops, block, dh), BF16),
                pltpu.VMEM((rows, wide), F32),
                pltpu.VMEM((2 * dh, rows), F32),
                pltpu.VMEM((2 * dh, rows), F32),
                pltpu.VMEM((hops, 2 * dh, rows), F32),
                pltpu.VMEM((hops, 2 * dh, rows), F32),
                pltpu.VMEM((hops, 2 * dh, rows), BF16),
                pltpu.VMEM((hops, 2 * dh, rows), BF16),
                dma((4,)),
                dma((hops,)), dma((hops,)),
                dma((hops,)), dma((hops,)),
                dma((hops,)), dma((hops,)),
                dma((hops,)), dma((hops,)),
            ],
            compiler_params=pltpu.CompilerParams(
                collective_id=0, has_side_effects=True, vmem_limit_bytes=56 << 20
            ),
        )(head_bias, doc_ids, query, keys, values, grad_out)

    split = P(("seq", "fold"), None)
    return jax.shard_map(
        body,
        mesh=mesh,
        in_specs=(split, split, split, split, P(), P(("seq", "fold"))),
        out_specs=(split, split, split),
        check_vma=False,
    )
```

```python
import functools
import math

import jax
import jax.numpy as jnp
from jax import lax
from jax.experimental import pallas as pl
from jax.experimental.pallas import tpu as pltpu
from jax.sharding import PartitionSpec as P

MAXDOC = 2048
MESH = pl.DeviceIdType.MESH
LOG2E = math.log2(math.e)
F32 = jnp.float32
BF16 = jnp.bfloat16


def dot_nt(a, b):
    return lax.dot_general(a, b, (((1,), (1,)), ((), ())), preferred_element_type=F32)


def dot_nn(a, b):
    return jnp.dot(a, b, preferred_element_type=F32)


def kernel(
    seq, fold, rows, dh, heads,
    bias_ref, ids_ref, query_ref, keys_ref, values_ref, grad_ref,
    out_query_ref, out_key_ref, out_value_ref,
    q_nat, q_tra, do_nat, do_tra, dom_nat, dom_tra, v_own,
    blocks, sib_blocks, acc, own_part, part_d, part_o, sib_part, ret_out, ret_in, aside_in,
    load_sem, fwd_send, fwd_recv, sib_send, sib_recv, sibp_send, sibp_recv, ret_send, ret_recv,
    aside_send, aside_recv,
):
    peers = seq * fold
    me = lax.axis_index("seq") * fold + lax.axis_index("fold")
    odd = lax.rem(me, 2)
    hops = MAXDOC // rows // 2
    factor = 1.0 / math.sqrt(dh)

    def device(index):
        index = lax.rem(index + peers, peers)
        return (index // fold, lax.rem(index, fold))

    sibling = device(me + 1 - 2 * odd)

    run = peers // 4

    def turns(index):
        return (index >= run) & (index < peers) & (lax.rem(index, run) < 2)

    turn = turns(me)
    turn_mate = turns(me - 2)
    turn_ahead = turns(me + 2)

    barrier = pltpu.get_barrier_semaphore()
    partners = jnp.int32(1)
    for hop in range(1, hops + 1):
        for far in (2 * hop, -2 * hop):
            valid = (me + far >= 0) & (me + far < peers)
            partners += valid.astype(jnp.int32)

            @pl.when(valid)
            def _():
                pl.semaphore_signal(
                    barrier, inc=1, device_id=device(me + far), device_id_type=MESH
                )

    pl.semaphore_signal(barrier, inc=1, device_id=sibling, device_id_type=MESH)

    cols = [pl.ds(h * dh, dh) for h in range(heads)]
    loads = [
        pltpu.make_async_copy(keys_ref, blocks.at[0, pl.ds(0, rows)], load_sem.at[0]),
        pltpu.make_async_copy(values_ref, v_own, load_sem.at[1]),
        pltpu.make_async_copy(query_ref, q_nat, load_sem.at[2]),
        pltpu.make_async_copy(grad_ref, do_nat, load_sem.at[3]),
    ]
    for load in loads:
        load.start()

    ids_row = ids_ref[...].astype(F32).reshape(1, rows)
    first = ids_row[:, 0:1]
    last = ids_row[:, rows - 1 : rows]
    ids_u = jnp.broadcast_to(ids_row, (rows, rows))
    ids_t = ids_u.T
    col_first = (ids_t[:, :dh] == first).astype(BF16)
    col_last = (ids_t[:, :dh] == last).astype(BF16)
    row_first = (ids_row == first).astype(BF16)
    row_last = (ids_row == last).astype(F32)

    chunks = (pl.ds(0, rows), pl.ds(rows, rows + 16))

    def push(src, dst, part, far, extra=0):
        slot = 2 * (dst - 1) + part
        return pltpu.make_async_remote_copy(
            blocks.at[src, chunks[part]], blocks.at[dst, chunks[part]],
            fwd_send.at[slot + extra], fwd_recv.at[slot],
            device_id=device(me + far), device_id_type=MESH,
        )

    def fwd(m, part):
        return push(0, m, part, 2 * m)

    def relay(m, part):
        return push(m, m + 2, part, 4)

    def sends(m):
        if m == 1:
            return (me + 2 < peers) & jnp.logical_not(turn_ahead)
        return me + 2 * m < peers

    def cross(part):
        return push(2, 1, part, -2, 2 * hops)

    def to_sib(m):
        slot = m - odd
        return pltpu.make_async_remote_copy(
            blocks.at[m], sib_blocks.at[slot], sib_send.at[slot], sib_recv.at[slot],
            device_id=sibling, device_id_type=MESH,
        )

    def part_to_sib(slot):
        return pltpu.make_async_remote_copy(
            part_o.at[slot], sib_part.at[slot], sibp_send.at[slot], sibp_recv.at[slot],
            device_id=sibling, device_id_type=MESH,
        )

    def ret(m):
        return pltpu.make_async_remote_copy(
            ret_out.at[m - 1], ret_in.at[m - 1], ret_send.at[m - 1], ret_recv.at[m - 1],
            device_id=device(me - 2 * m), device_id_type=MESH,
        )

    loads[0].wait()
    pl.semaphore_wait(barrier, partners)
    for m in (1, 2):
        pl.when(sends(m))(fwd(m, 0).start)
    loads[1].wait()
    blocks[0, pl.ds(rows, rows)] = v_own[...] * col_last
    blocks[0, pl.ds(2 * rows, 16)] = jnp.broadcast_to(last, (16, dh)).astype(BF16)
    for m in (1, 2):
        pl.when(sends(m))(fwd(m, 1).start)

    @pl.when(odd == 0)
    def _():
        to_sib(0).start()

    loads[2].wait()
    loads[3].wait()
    for h in range(heads):
        q_tra[cols[h], :] = q_nat[:, cols[h]].T
        do_tra[cols[h], :] = do_nat[:, cols[h]].T
    for h in range(heads):
        dom_nat[:, cols[h]] = do_nat[:, cols[h]] * col_first
        dom_tra[cols[h], :] = do_tra[cols[h], :] * row_first

    def block(k, v, g_nat, g_tra, mask):
        def scores(h):
            return dot_nt(q_nat[:, cols[h]], k), dot_nt(g_nat[:, cols[h]], v)

        grad_k = jnp.zeros((dh, rows), F32)
        grad_v = jnp.zeros((dh, rows), F32)
        ahead = scores(0)
        for h in range(heads):
            s, dp = ahead
            if h + 1 < heads:
                ahead = scores(h + 1)
            grow = jnp.exp2(s * (-factor * LOG2E) + bias_ref[h] * (-LOG2E))
            p = 1.0 / (1.0 + grow)
            if mask is not None:
                p = p * mask
            ds = (dp * (p * (1.0 - p))).astype(BF16)
            p = p.astype(BF16)
            acc[:, cols[h]] += dot_nn(ds, k)
            grad_v = grad_v + dot_nn(g_tra[cols[h], :], p)
            grad_k = grad_k + dot_nn(q_tra[cols[h], :], ds)
        return grad_k, grad_v

    acc[...] = jnp.zeros(acc.shape, F32)

    def own_block():
        iota_t = lax.broadcasted_iota(jnp.int32, (rows, rows), 0)
        iota_u = lax.broadcasted_iota(jnp.int32, (rows, rows), 1)
        mask = ((ids_t == ids_u) & (iota_u <= iota_t)).astype(F32)
        grad_k, grad_v = block(blocks[0, pl.ds(0, rows)], v_own[...], do_nat, do_tra, mask)
        own_part[pl.ds(0, dh)] = grad_k
        own_part[pl.ds(dh, dh)] = grad_v

    def relays(m):
        return (m <= 2) & (me >= 2 * m) & (me + 4 < peers)

    def arrived(m, part):
        pl.when(me >= 2 * m)(fwd(m, part).wait_recv)

        @pl.when(me < 2 * m)
        def _():
            blocks[m, chunks[part]] = jnp.full((rows + 16 * part, dh), -1.0, BF16)

        @pl.when(relays(m))
        def _():
            relay(m, part).start()

        @pl.when((m == 2) & turn_mate)
        def _():
            cross(part).start()

    def far_block(ref, part):
        gate = (ref[pl.ds(2 * rows, 16)][0:1].astype(F32) == first).astype(F32)
        k = ref[pl.ds(0, rows)]
        v = ref[pl.ds(rows, rows)] * gate.astype(BF16)
        grad_k, grad_v = block(k, v, dom_nat, dom_tra, None)
        part[pl.ds(0, dh)] = grad_k
        part[pl.ds(dh, dh)] = grad_v * jnp.concatenate([gate] * (rows // dh), axis=1)

    def order(step):
        return step + 2 - 2 * lax.rem(step, 2)

    def aside():
        return pltpu.make_async_remote_copy(
            ret_out.at[0], aside_in, aside_send, aside_recv,
            device_id=device(me + 2), device_id_type=MESH,
        )

    def send_back(m):
        back = m - odd

        @pl.when(back < hops)
        def _():
            part_to_sib(back).wait_recv()
            ret_out[m - 1] = (part_d[m - 1] + sib_part[back]).astype(BF16)

        @pl.when(back >= hops)
        def _():
            ret_out[m - 1] = part_d[m - 1].astype(BF16)

        @pl.when((m == 2) & turn_mate)
        def _():
            aside().wait_recv()
            ret_out[1] = (ret_out[1].astype(F32) + aside_in[...].astype(F32)).astype(BF16)

        pl.when((m == 1) & turn)(aside().start)
        pl.when((me >= 2 * m) & jnp.logical_not((m == 1) & turn))(ret(m).start)

    def body(step, carry):
        m = order(step)
        slot = lax.rem(m - 1 + odd, hops)
        pl.when(step != 1)(functools.partial(arrived, m, 0))
        arrived(m, 1)

        @pl.when(m - odd < hops)
        def _():
            to_sib(m).start()

        far_block(blocks.at[m], part_d.at[m - 1])

        @pl.when((step > 0) & jnp.logical_not((step == 1) & turn_mate))
        def _():
            send_back(order(step - 1))

        to_sib(slot + odd).wait_recv()
        far_block(sib_blocks.at[slot], part_o.at[slot])
        part_to_sib(slot).start()

        @pl.when(step == 0)
        def _():
            arrived(order(1), 0)
            own_block()

        return carry

    lax.fori_loop(0, hops, body, 0)

    out_query_ref[...] = (acc[...] * factor).astype(BF16)
    send_back(order(hops - 1))

    @pl.when(turn_mate)
    def _():
        send_back(jnp.int32(2))

    @pl.when(odd == 0)
    def _():
        part_to_sib(0).wait_recv()
        own_part[...] = own_part[...] + sib_part[0] * row_last

    for m in (2, 1, 4, 3):

        @pl.when(sends(m))
        def _():
            ret(m).wait_recv()
            own_part[...] = own_part[...] + ret_in[m - 1].astype(F32) * row_last

    out_key_ref[...] = (own_part[pl.ds(0, dh)] * factor).T.astype(BF16)
    out_value_ref[...] = own_part[pl.ds(dh, dh)].T.astype(BF16)
    for m in range(1, hops + 1):
        if m <= 2:
            for part in (0, 1):
                pl.when(sends(m))(fwd(m, part).wait_send)
                pl.when(relays(m))(relay(m, part).wait_send)
        if m == 1:
            pl.when((me >= 2) & jnp.logical_not(turn))(ret(m).wait_send)
            pl.when(turn)(aside().wait_send)
        else:
            pl.when(me >= 2 * m)(ret(m).wait_send)
        if m == 2:
            for part in (0, 1):
                pl.when(turn_mate)(cross(part).wait_send)
        part_to_sib(m - 1).wait_send()
    for slot in range(hops):
        to_sib(slot + odd).wait_send()


def hand_on(q_in, k_in, v_in, q_out, k_out, v_out, sem):
    copies = [
        pltpu.make_async_copy(src, dst, sem.at[i])
        for i, (src, dst) in enumerate(((q_in, q_out), (k_in, k_out), (v_in, v_out)))
    ]
    for copy in copies:
        copy.start()
    for copy in copies:
        copy.wait()


def solution(mesh):
    seq, fold = mesh.shape["seq"], mesh.shape["fold"]

    def body(query, keys, values, grad_out, head_bias, doc_ids):
        rows, dh = keys.shape
        heads = query.shape[1] // dh
        hops = MAXDOC // rows // 2
        wide = heads * dh
        block = 2 * rows + 16
        vmem = pl.BlockSpec(memory_space=pltpu.VMEM)
        hbm = pl.BlockSpec(memory_space=pl.ANY)
        dma = pltpu.SemaphoreType.DMA
        shapes = (
            jax.ShapeDtypeStruct((rows, wide), BF16),
            jax.ShapeDtypeStruct((rows, dh), BF16),
            jax.ShapeDtypeStruct((rows, dh), BF16),
        )
        grads = pl.pallas_call(
            functools.partial(kernel, seq, fold, rows, dh, heads),
            out_shape=tuple(pltpu.VMEM(x.shape, x.dtype) for x in shapes),
            in_specs=[pl.BlockSpec(memory_space=pltpu.SMEM), vmem, hbm, hbm, hbm, hbm],
            out_specs=(vmem, vmem, vmem),
            scratch_shapes=[
                pltpu.VMEM((rows, wide), BF16),
                pltpu.VMEM((wide, rows), BF16),
                pltpu.VMEM((rows, wide), BF16),
                pltpu.VMEM((wide, rows), BF16),
                pltpu.VMEM((rows, wide), BF16),
                pltpu.VMEM((wide, rows), BF16),
                pltpu.VMEM((rows, dh), BF16),
                pltpu.VMEM((hops + 1, block, dh), BF16),
                pltpu.VMEM((hops, block, dh), BF16),
                pltpu.VMEM((rows, wide), F32),
                pltpu.VMEM((2 * dh, rows), F32),
                pltpu.VMEM((hops, 2 * dh, rows), F32),
                pltpu.VMEM((hops, 2 * dh, rows), F32),
                pltpu.VMEM((hops, 2 * dh, rows), F32),
                pltpu.VMEM((hops, 2 * dh, rows), BF16),
                pltpu.VMEM((hops, 2 * dh, rows), BF16),
                pltpu.VMEM((2 * dh, rows), BF16),
                dma((4,)),
                dma((2 * hops + 2,)), dma((2 * hops,)),
                dma((hops,)), dma((hops,)),
                dma((hops,)), dma((hops,)),
                dma((hops,)), dma((hops,)),
                dma, dma,
            ],
            compiler_params=pltpu.CompilerParams(
                collective_id=0, has_side_effects=True, vmem_limit_bytes=58 << 20
            ),
        )(head_bias, doc_ids, query, keys, values, grad_out)
        return pl.pallas_call(
            hand_on,
            out_shape=shapes,
            in_specs=[vmem] * 3,
            out_specs=(hbm,) * 3,
            scratch_shapes=[dma((3,))],
            compiler_params=pltpu.CompilerParams(vmem_limit_bytes=1 << 20),
        )(*grads)

    split = P(("seq", "fold"), None)
    return jax.shard_map(
        body,
        mesh=mesh,
        in_specs=(split, split, split, split, P(), P(("seq", "fold"))),
        out_specs=(split, split, split),
        check_vma=False,
    )
```

```python
import functools
import math

import jax
import jax.numpy as jnp
from jax import lax
from jax.experimental import pallas as pl
from jax.experimental.pallas import tpu as pltpu
from jax.sharding import PartitionSpec as P

MAXDOC = 2048
MESH = pl.DeviceIdType.MESH
LOG2E = math.log2(math.e)
F32 = jnp.float32
BF16 = jnp.bfloat16


def dot_nt(a, b):
    return lax.dot_general(a, b, (((1,), (1,)), ((), ())), preferred_element_type=F32)


def dot_nn(a, b):
    return jnp.dot(a, b, preferred_element_type=F32)


def kernel(
    seq, fold, rows, dh, heads,
    bias_ref, ids_ref, query_ref, keys_ref, values_ref, grad_ref,
    out_query_ref, out_key_ref, out_value_ref,
    q_nat, q_tra, do_nat, do_tra, dom_nat, dom_tra, v_own,
    blocks, sib_blocks, acc, own_part, part_d, part_o, sib_part, ret_out, ret_in, aside_in,
    load_sem, fwd_send, fwd_recv, sib_send, sib_recv, sibp_send, sibp_recv, ret_send, ret_recv,
    aside_send, aside_recv,
):
    peers = seq * fold
    me = lax.axis_index("seq") * fold + lax.axis_index("fold")
    odd = lax.rem(me, 2)
    hops = MAXDOC // rows // 2
    half = rows // 2
    factor = 1.0 / math.sqrt(dh)
    run = peers // 4

    def device(index):
        index = lax.rem(index + peers, peers)
        return (index // fold, lax.rem(index, fold))

    def turns(index):
        return (index >= run) & (index < peers) & (lax.rem(index, run) < 2)

    sibling = device(me + 1 - 2 * odd)
    turn = turns(me)
    turn_mate = turns(me - 2)
    turn_ahead = turns(me + 2)

    barrier = pltpu.get_barrier_semaphore()
    partners = jnp.int32(1)
    for hop in range(1, hops + 1):
        for far in (2 * hop, -2 * hop):
            valid = (me + far >= 0) & (me + far < peers)
            partners += valid.astype(jnp.int32)

            @pl.when(valid)
            def _():
                pl.semaphore_signal(
                    barrier, inc=1, device_id=device(me + far), device_id_type=MESH
                )

    pl.semaphore_signal(barrier, inc=1, device_id=sibling, device_id_type=MESH)

    cols = [pl.ds(h * dh, dh) for h in range(heads)]
    parts = [pl.ds(c * half, half) for c in (0, 1)]
    k_rows, v_rows, id_rows = pl.ds(0, half), pl.ds(half, half), pl.ds(rows, 16)
    loads = [
        pltpu.make_async_copy(keys_ref.at[parts[0]], blocks.at[0, 0, k_rows], load_sem.at[0]),
        pltpu.make_async_copy(keys_ref.at[parts[1]], blocks.at[0, 1, k_rows], load_sem.at[1]),
        pltpu.make_async_copy(values_ref, v_own, load_sem.at[2]),
        pltpu.make_async_copy(query_ref, q_nat, load_sem.at[3]),
        pltpu.make_async_copy(grad_ref, do_nat, load_sem.at[4]),
    ]
    for load in loads:
        load.start()

    ids_row = ids_ref[...].astype(F32).reshape(1, rows)
    first = ids_row[:, 0:1]
    last = ids_row[:, rows - 1 : rows]
    ids_u = jnp.broadcast_to(ids_row, (rows, rows))
    ids_t = ids_u.T
    col_first = (ids_t[:, :dh] == first).astype(BF16)
    col_last = (ids_t[:, :dh] == last).astype(BF16)
    row_first = (ids_row == first).astype(BF16)
    row_last = (ids_row == last).astype(F32)

    def push(src, dst, c, far, extra=0):
        slot = 2 * (dst - 1) + c
        return pltpu.make_async_remote_copy(
            blocks.at[src, c], blocks.at[dst, c],
            fwd_send.at[slot + extra], fwd_recv.at[slot],
            device_id=device(me + far), device_id_type=MESH,
        )

    def fwd(m, c):
        return push(0, m, c, 2 * m)

    def relay(m, c):
        return push(m, m + 2, c, 4)

    def cross(c):
        return push(2, 1, c, -2, 2 * hops)

    def sends(m, c):
        if m == 1 and c == 0:
            return (me + 2 < peers) & jnp.logical_not(turn_ahead)
        return me + 2 * m < peers

    def returns(m):
        if m == 1:
            return (me + 2 < peers) & jnp.logical_not(turn_ahead)
        return me + 2 * m < peers

    def relays(m):
        return (me >= 2 * m) & (me + 4 < peers)

    def to_sib(m, c):
        slot = m - odd
        return pltpu.make_async_remote_copy(
            blocks.at[m, c], sib_blocks.at[slot, c],
            sib_send.at[2 * slot + c], sib_recv.at[2 * slot + c],
            device_id=sibling, device_id_type=MESH,
        )

    def part_to_sib(slot, c):
        return pltpu.make_async_remote_copy(
            part_o.at[slot, c], sib_part.at[slot, c],
            sibp_send.at[2 * slot + c], sibp_recv.at[2 * slot + c],
            device_id=sibling, device_id_type=MESH,
        )

    def ret(m, c):
        slot = 2 * (m - 1) + c
        return pltpu.make_async_remote_copy(
            ret_out.at[m - 1, c], ret_in.at[m - 1, c], ret_send.at[slot], ret_recv.at[slot],
            device_id=device(me - 2 * m), device_id_type=MESH,
        )

    def aside(c):
        return pltpu.make_async_remote_copy(
            ret_out.at[0, c], aside_in.at[c], aside_send.at[c], aside_recv.at[c],
            device_id=device(me + 2), device_id_type=MESH,
        )

    for load in loads[:3]:
        load.wait()
    for c in (0, 1):
        blocks[0, c, v_rows] = v_own[parts[c]] * col_last[c * half : c * half + half]
        blocks[0, c, id_rows] = jnp.broadcast_to(last, (16, dh)).astype(BF16)
    pl.semaphore_wait(barrier, partners)
    for c in (0, 1):
        for m in (1, 2):
            pl.when(sends(m, c))(fwd(m, c).start)

    @pl.when(odd == 0)
    def _():
        for c in (0, 1):
            to_sib(0, c).start()

    for load in loads[3:]:
        load.wait()
    for h in range(heads):
        q_tra[cols[h], :] = q_nat[:, cols[h]].T
        do_tra[cols[h], :] = do_nat[:, cols[h]].T
    for h in range(heads):
        dom_nat[:, cols[h]] = do_nat[:, cols[h]] * col_first
        dom_tra[cols[h], :] = do_tra[cols[h], :] * row_first

    def block(k, v, g_nat, g_tra, mask):
        def scores(h):
            return dot_nt(q_nat[:, cols[h]], k), dot_nt(g_nat[:, cols[h]], v)

        grad_k = jnp.zeros((dh, rows), F32)
        grad_v = jnp.zeros((dh, rows), F32)
        ahead = scores(0)
        for h in range(heads):
            s, dp = ahead
            if h + 1 < heads:
                ahead = scores(h + 1)
            grow = jnp.exp2(s * (-factor * LOG2E) + bias_ref[h] * (-LOG2E))
            p = 1.0 / (1.0 + grow)
            if mask is not None:
                p = p * mask
            ds = (dp * (p * (1.0 - p))).astype(BF16)
            p = p.astype(BF16)
            if mask is not None:
                acc[:, cols[h]] = dot_nn(ds, k)
            else:
                acc[:, cols[h]] += dot_nn(ds, k)
            grad_v = grad_v + dot_nn(g_tra[cols[h], :], p)
            grad_k = grad_k + dot_nn(q_tra[cols[h], :], ds)
        return grad_k, grad_v

    iota_t = lax.broadcasted_iota(jnp.int32, (rows, rows), 0)
    iota_u = lax.broadcasted_iota(jnp.int32, (rows, rows), 1)
    own_mask = ((ids_t == ids_u) & (iota_u <= iota_t)).astype(F32)
    own_k = jnp.concatenate([blocks[0, c, k_rows] for c in (0, 1)], axis=0)
    grad_k, grad_v = block(own_k, v_own[...], do_nat, do_tra, own_mask)
    own_part[pl.ds(0, dh)] = grad_k
    own_part[pl.ds(dh, dh)] = grad_v

    def arrived(m, c):
        pl.when(me >= 2 * m)(fwd(m, c).wait_recv)

        @pl.when(me < 2 * m)
        def _():
            blocks[m, c] = jnp.full((rows + 16, dh), -1.0, BF16)

        if m <= 2:
            pl.when(relays(m))(relay(m, c).start)
        if m == 2 and c == 0:
            pl.when(turn_mate)(cross(c).start)
        pl.when(m - odd < hops)(to_sib(m, c).start)

    def far_blocks(m, slot, c):
        refs = (blocks.at[m, c], sib_blocks.at[slot, c])
        gates = [(ref[id_rows][0:1].astype(F32) == first).astype(F32) for ref in refs]
        k = jnp.concatenate([ref[k_rows] for ref in refs], axis=0)
        v = jnp.concatenate(
            [ref[v_rows] * gate.astype(BF16) for ref, gate in zip(refs, gates)], axis=0
        )
        grad_k, grad_v = block(k, v, dom_nat, dom_tra, None)
        grad_v = grad_v * jnp.concatenate(gates, axis=1)
        part_d[m - 1, c, pl.ds(0, dh)] = grad_k[:, :half]
        part_d[m - 1, c, pl.ds(dh, dh)] = grad_v[:, :half]
        part_o[slot, c, pl.ds(0, dh)] = grad_k[:, half:]
        part_o[slot, c, pl.ds(dh, dh)] = grad_v[:, half:]

    def send_back(m, c):
        back = m - odd

        @pl.when(back < hops)
        def _():
            part_to_sib(back, c).wait_recv()
            ret_out[m - 1, c] = (part_d[m - 1, c] + sib_part[back, c]).astype(BF16)

        @pl.when(back >= hops)
        def _():
            ret_out[m - 1, c] = part_d[m - 1, c].astype(BF16)

        if m == 2:

            @pl.when(turn_mate)
            def _():
                aside(c).wait_recv()
                ret_out[1, c] = (
                    ret_out[1, c].astype(F32) + aside_in[c].astype(F32)
                ).astype(BF16)

        if m == 1:
            pl.when(turn)(aside(c).start)
            pl.when((me >= 2) & jnp.logical_not(turn))(ret(m, c).start)
        else:
            pl.when(me >= 2 * m)(ret(m, c).start)

    def send_back_far(m, c):
        if m == 2:
            pl.when(jnp.logical_not(turn_mate))(functools.partial(send_back, m, c))
        else:
            send_back(m, c)

    order = ((2, 0), (2, 1), (1, 0), (4, 0), (1, 1), (3, 0), (4, 1), (3, 1))
    after = {
        0: (((1, 0),), ()),
        1: (((4, 0),), ((2, 0),)),
        2: (((1, 1),), ((2, 1),)),
        3: (((3, 0), (4, 1)), ((1, 0),)),
        4: ((), ((4, 0),)),
        5: (((3, 1),), ((1, 1),)),
        6: ((), ((3, 0),)),
        7: ((), ((4, 1),)),
    }

    arrived(2, 0)
    arrived(2, 1)

    def body(step, carry):
        m, c = jnp.int32(0), jnp.int32(0)
        for i, (far, part) in enumerate(order):
            here = (step == i).astype(jnp.int32)
            m += far * here
            c += part * here
        slot = lax.rem(m - 1 + odd, hops)
        to_sib(slot + odd, c).wait_recv()
        far_blocks(m, slot, c)
        part_to_sib(slot, c).start()

        for i, (fresh, done) in after.items():

            @pl.when(step == i)
            def _():
                for pair in done:
                    send_back_far(*pair)
                for pair in fresh:
                    arrived(*pair)

        return carry

    lax.fori_loop(0, len(order), body, 0)

    out_query_ref[...] = (acc[...] * factor).astype(BF16)
    send_back(3, 1)

    @pl.when(turn_mate)
    def _():
        for c in (0, 1):
            send_back(2, c)

    @pl.when(odd == 0)
    def _():
        for c in (0, 1):
            part_to_sib(0, c).wait_recv()
            own_part[:, parts[c]] += sib_part[0, c] * row_last[:, c * half : c * half + half]

    for m in (2, 1, 4, 3):
        for c in (0, 1):

            @pl.when(returns(m))
            def _():
                ret(m, c).wait_recv()
                own_part[:, parts[c]] += (
                    ret_in[m - 1, c].astype(F32) * row_last[:, c * half : c * half + half]
                )

    out_key_ref[...] = (own_part[pl.ds(0, dh)] * factor).T.astype(BF16)
    out_value_ref[...] = own_part[pl.ds(dh, dh)].T.astype(BF16)

    for c in (0, 1):
        for m in (1, 2):
            pl.when(sends(m, c))(fwd(m, c).wait_send)
            pl.when(relays(m))(relay(m, c).wait_send)
        if c == 0:
            pl.when(turn_mate)(cross(c).wait_send)
        pl.when(turn)(aside(c).wait_send)
        pl.when((me >= 2) & jnp.logical_not(turn))(ret(1, c).wait_send)
        for m in range(2, hops + 1):
            pl.when(me >= 2 * m)(ret(m, c).wait_send)
        for slot in range(hops):
            part_to_sib(slot, c).wait_send()
            to_sib(slot + odd, c).wait_send()


def hand_on(q_in, k_in, v_in, q_out, k_out, v_out, sem):
    copies = [
        pltpu.make_async_copy(src, dst, sem.at[i])
        for i, (src, dst) in enumerate(((q_in, q_out), (k_in, k_out), (v_in, v_out)))
    ]
    for copy in copies:
        copy.start()
    for copy in copies:
        copy.wait()


def solution(mesh):
    seq, fold = mesh.shape["seq"], mesh.shape["fold"]

    def body(query, keys, values, grad_out, head_bias, doc_ids):
        rows, dh = keys.shape
        heads = query.shape[1] // dh
        hops = MAXDOC // rows // 2
        wide = heads * dh
        block = rows + 16
        vmem = pl.BlockSpec(memory_space=pltpu.VMEM)
        hbm = pl.BlockSpec(memory_space=pl.ANY)
        dma = pltpu.SemaphoreType.DMA
        shapes = (
            jax.ShapeDtypeStruct((rows, wide), BF16),
            jax.ShapeDtypeStruct((rows, dh), BF16),
            jax.ShapeDtypeStruct((rows, dh), BF16),
        )
        grads = pl.pallas_call(
            functools.partial(kernel, seq, fold, rows, dh, heads),
            out_shape=tuple(pltpu.VMEM(x.shape, x.dtype) for x in shapes),
            in_specs=[pl.BlockSpec(memory_space=pltpu.SMEM), vmem, hbm, hbm, hbm, hbm],
            out_specs=(vmem, vmem, vmem),
            scratch_shapes=[
                pltpu.VMEM((rows, wide), BF16),
                pltpu.VMEM((wide, rows), BF16),
                pltpu.VMEM((rows, wide), BF16),
                pltpu.VMEM((wide, rows), BF16),
                pltpu.VMEM((rows, wide), BF16),
                pltpu.VMEM((wide, rows), BF16),
                pltpu.VMEM((rows, dh), BF16),
                pltpu.VMEM((hops + 1, 2, block, dh), BF16),
                pltpu.VMEM((hops, 2, block, dh), BF16),
                pltpu.VMEM((rows, wide), F32),
                pltpu.VMEM((2 * dh, rows), F32),
                pltpu.VMEM((hops, 2, 2 * dh, rows // 2), F32),
                pltpu.VMEM((hops, 2, 2 * dh, rows // 2), F32),
                pltpu.VMEM((hops, 2, 2 * dh, rows // 2), F32),
                pltpu.VMEM((hops, 2, 2 * dh, rows // 2), BF16),
                pltpu.VMEM((hops, 2, 2 * dh, rows // 2), BF16),
                pltpu.VMEM((2, 2 * dh, rows // 2), BF16),
                dma((5,)),
                dma((2 * hops + 2,)), dma((2 * hops,)),
                dma((2 * hops,)), dma((2 * hops,)),
                dma((2 * hops,)), dma((2 * hops,)),
                dma((2 * hops,)), dma((2 * hops,)),
                dma((2,)), dma((2,)),
            ],
            compiler_params=pltpu.CompilerParams(
                collective_id=0, has_side_effects=True, vmem_limit_bytes=58 << 20
            ),
        )(head_bias, doc_ids, query, keys, values, grad_out)
        return pl.pallas_call(
            hand_on,
            out_shape=shapes,
            in_specs=[vmem] * 3,
            out_specs=(hbm,) * 3,
            scratch_shapes=[dma((3,))],
            compiler_params=pltpu.CompilerParams(vmem_limit_bytes=1 << 20),
        )(*grads)

    split = P(("seq", "fold"), None)
    return jax.shard_map(
        body,
        mesh=mesh,
        in_specs=(split, split, split, split, P(), P(("seq", "fold"))),
        out_specs=(split, split, split),
        check_vma=False,
    )
```

```python
import functools
import math

import jax
import jax.numpy as jnp
from jax import lax
from jax.experimental import pallas as pl
from jax.experimental.pallas import tpu as pltpu
from jax.sharding import PartitionSpec as P

MAXDOC = 2048
MESH = pl.DeviceIdType.MESH
LOG2E = math.log2(math.e)
F32 = jnp.float32
BF16 = jnp.bfloat16


def dot_nt(a, b):
    return lax.dot_general(a, b, (((1,), (1,)), ((), ())), preferred_element_type=F32)


def dot_nn(a, b):
    return jnp.dot(a, b, preferred_element_type=F32)


def kernel(
    seq, fold, rows, dh, heads,
    bias_hbm, ids_hbm, query_ref, keys_ref, values_ref, grad_ref,
    out_query_ref, out_key_ref, out_value_ref,
    q_nat, q_tra, do_nat, do_tra, dom_nat, dom_tra, v_own,
    blocks, sib_blocks, acc, own_part, part_d, part_o, sib_part, ret_out, ret_in, aside_in,
    bias_ref, ids_ref, load_sem, fwd_send, fwd_recv, sib_send, sib_recv, sibp_send, sibp_recv, ret_send, ret_recv,
    aside_send, aside_recv,
):
    peers = seq * fold
    me = lax.axis_index("seq") * fold + lax.axis_index("fold")
    odd = lax.rem(me, 2)
    hops = MAXDOC // rows // 2
    half = rows // 2
    factor = 1.0 / math.sqrt(dh)
    run = peers // 4

    def device(index):
        index = lax.rem(index + peers, peers)
        return (index // fold, lax.rem(index, fold))

    def turns(index):
        return (index >= run) & (index < peers) & (lax.rem(index, run) < 2)

    sibling = device(me + 1 - 2 * odd)
    turn = turns(me)
    turn_mate = turns(me - 2)
    turn_ahead = turns(me + 2)

    cols = [pl.ds(h * dh, dh) for h in range(heads)]
    parts = [pl.ds(c * half, half) for c in (0, 1)]
    k_rows, v_rows, id_rows = pl.ds(0, half), pl.ds(half, half), pl.ds(rows, 16)
    loads = [
        pltpu.make_async_copy(keys_ref.at[parts[0]], blocks.at[0, 0, k_rows], load_sem.at[0]),
        pltpu.make_async_copy(keys_ref.at[parts[1]], blocks.at[0, 1, k_rows], load_sem.at[1]),
        pltpu.make_async_copy(values_ref, v_own, load_sem.at[2]),
        pltpu.make_async_copy(ids_hbm, ids_ref, load_sem.at[3]),
        pltpu.make_async_copy(bias_hbm, bias_ref, load_sem.at[4]),
        pltpu.make_async_copy(query_ref, q_nat, load_sem.at[5]),
        pltpu.make_async_copy(grad_ref, do_nat, load_sem.at[6]),
    ]
    for load in loads:
        load.start()

    barrier = pltpu.get_barrier_semaphore()
    partners = jnp.int32(1)
    for hop in range(1, hops + 1):
        for far in (2 * hop, -2 * hop):
            valid = (me + far >= 0) & (me + far < peers)
            partners += valid.astype(jnp.int32)

            @pl.when(valid)
            def _():
                pl.semaphore_signal(
                    barrier, inc=1, device_id=device(me + far), device_id_type=MESH
                )

    pl.semaphore_signal(barrier, inc=1, device_id=sibling, device_id_type=MESH)

    loads[3].wait()

    ids_row = ids_ref[...].astype(F32).reshape(1, rows)
    first = ids_row[:, 0:1]
    last = ids_row[:, rows - 1 : rows]
    ids_u = jnp.broadcast_to(ids_row, (rows, rows))
    ids_t = ids_u.T
    col_first = (ids_t[:, :dh] == first).astype(BF16)
    col_last = (ids_t[:, :dh] == last).astype(BF16)
    row_first = (ids_row == first).astype(BF16)
    row_last = (ids_row == last).astype(F32)

    def push(src, dst, c, far, extra=0):
        slot = 2 * (dst - 1) + c
        return pltpu.make_async_remote_copy(
            blocks.at[src, c], blocks.at[dst, c],
            fwd_send.at[slot + extra], fwd_recv.at[slot],
            device_id=device(me + far), device_id_type=MESH,
        )

    def fwd(m, c):
        return push(0, m, c, 2 * m)

    def relay(m, c):
        return push(m, m + 2, c, 4)

    def cross(c):
        return push(2, 1, c, -2, 2 * hops)

    def sends(m, c):
        if m == 1 and c == 0:
            return (me + 2 < peers) & jnp.logical_not(turn_ahead)
        return me + 2 * m < peers

    def returns(m, c):
        if m == 1 and c == 1:
            return (me + 2 < peers) & jnp.logical_not(turn_ahead)
        return me + 2 * m < peers

    def relays(m):
        return (me >= 2 * m) & (me + 4 < peers)

    def to_sib(m, c):
        slot = m - odd
        return pltpu.make_async_remote_copy(
            blocks.at[m, c], sib_blocks.at[slot, c],
            sib_send.at[2 * slot + c], sib_recv.at[2 * slot + c],
            device_id=sibling, device_id_type=MESH,
        )

    def part_to_sib(slot, c):
        return pltpu.make_async_remote_copy(
            part_o.at[slot, c], sib_part.at[slot, c],
            sibp_send.at[2 * slot + c], sibp_recv.at[2 * slot + c],
            device_id=sibling, device_id_type=MESH,
        )

    def ret(m, c):
        slot = 2 * (m - 1) + c
        return pltpu.make_async_remote_copy(
            ret_out.at[m - 1, c], ret_in.at[m - 1, c], ret_send.at[slot], ret_recv.at[slot],
            device_id=device(me - 2 * m), device_id_type=MESH,
        )

    def aside(c):
        return pltpu.make_async_remote_copy(
            ret_out.at[0, c], aside_in.at[c], aside_send.at[c], aside_recv.at[c],
            device_id=device(me + 2), device_id_type=MESH,
        )

    for load in loads[:3]:
        load.wait()
    for c in (0, 1):
        blocks[0, c, v_rows] = v_own[parts[c]] * col_last[c * half : c * half + half]
        blocks[0, c, id_rows] = jnp.broadcast_to(last, (16, dh)).astype(BF16)
    pl.semaphore_wait(barrier, partners)
    for c in (0, 1):
        for m in (1, 2):
            pl.when(sends(m, c))(fwd(m, c).start)

    @pl.when(odd == 0)
    def _():
        for c in (0, 1):
            to_sib(0, c).start()

    for load in loads[4:]:
        load.wait()
    for h in range(heads):
        q_tra[cols[h], :] = q_nat[:, cols[h]].T
        do_tra[cols[h], :] = do_nat[:, cols[h]].T
    for h in range(heads):
        dom_nat[:, cols[h]] = do_nat[:, cols[h]] * col_first
        dom_tra[cols[h], :] = do_tra[cols[h], :] * row_first

    def block(k, v, g_nat, g_tra, mask):
        def scores(h):
            return dot_nt(q_nat[:, cols[h]], k), dot_nt(g_nat[:, cols[h]], v)

        grad_k = jnp.zeros((dh, rows), F32)
        grad_v = jnp.zeros((dh, rows), F32)
        ahead = scores(0)
        for h in range(heads):
            s, dp = ahead
            if h + 1 < heads:
                ahead = scores(h + 1)
            grow = jnp.exp2(s * (-factor * LOG2E) + bias_ref[h] * (-LOG2E))
            p = 1.0 / (1.0 + grow)
            if mask is not None:
                p = p * mask
            ds = (dp * (p * (1.0 - p))).astype(BF16)
            p = p.astype(BF16)
            if mask is not None:
                acc[:, cols[h]] = dot_nn(ds, k)
            else:
                acc[:, cols[h]] += dot_nn(ds, k)
            grad_v = grad_v + dot_nn(g_tra[cols[h], :], p)
            grad_k = grad_k + dot_nn(q_tra[cols[h], :], ds)
        return grad_k, grad_v

    iota_t = lax.broadcasted_iota(jnp.int32, (rows, rows), 0)
    iota_u = lax.broadcasted_iota(jnp.int32, (rows, rows), 1)
    own_mask = ((ids_t == ids_u) & (iota_u <= iota_t)).astype(F32)
    own_k = jnp.concatenate([blocks[0, c, k_rows] for c in (0, 1)], axis=0)
    grad_k, grad_v = block(own_k, v_own[...], do_nat, do_tra, own_mask)
    own_part[pl.ds(0, dh)] = grad_k
    own_part[pl.ds(dh, dh)] = grad_v

    def arrived(m, c):
        pl.when(me >= 2 * m)(fwd(m, c).wait_recv)

        @pl.when(me < 2 * m)
        def _():
            blocks[m, c] = jnp.full((rows + 16, dh), -1.0, BF16)

        if m <= 2:
            pl.when(relays(m))(relay(m, c).start)
        if m == 2 and c == 0:
            pl.when(turn_mate)(cross(c).start)
        pl.when(m - odd < hops)(to_sib(m, c).start)

    def far_blocks(m, slot, c):
        refs = (blocks.at[m, c], sib_blocks.at[slot, c])
        gates = [(ref[id_rows][0:1].astype(F32) == first).astype(F32) for ref in refs]
        k = jnp.concatenate([ref[k_rows] for ref in refs], axis=0)
        v = jnp.concatenate(
            [ref[v_rows] * gate.astype(BF16) for ref, gate in zip(refs, gates)], axis=0
        )
        grad_k, grad_v = block(k, v, dom_nat, dom_tra, None)
        grad_v = grad_v * jnp.concatenate(gates, axis=1)
        part_d[m - 1, c, pl.ds(0, dh)] = grad_k[:, :half]
        part_d[m - 1, c, pl.ds(dh, dh)] = grad_v[:, :half]
        part_o[slot, c, pl.ds(0, dh)] = grad_k[:, half:]
        part_o[slot, c, pl.ds(dh, dh)] = grad_v[:, half:]

    def send_back(m, c):
        back = m - odd

        @pl.when(back < hops)
        def _():
            part_to_sib(back, c).wait_recv()
            ret_out[m - 1, c] = (part_d[m - 1, c] + sib_part[back, c]).astype(BF16)

        @pl.when(back >= hops)
        def _():
            ret_out[m - 1, c] = part_d[m - 1, c].astype(BF16)

        if m == 2 and c == 1:

            @pl.when(turn_mate)
            def _():
                aside(c).wait_recv()
                ret_out[1, c] = (
                    ret_out[1, c].astype(F32) + aside_in[c].astype(F32)
                ).astype(BF16)

        if m == 1 and c == 1:
            pl.when(turn)(aside(c).start)
            pl.when((me >= 2) & jnp.logical_not(turn))(ret(m, c).start)
        else:
            pl.when(me >= 2 * m)(ret(m, c).start)

    def send_back_far(m, c):
        if m == 2 and c == 1:
            pl.when(jnp.logical_not(turn_mate))(functools.partial(send_back, m, c))
        else:
            send_back(m, c)

    order = ((2, 0), (2, 1), (1, 0), (4, 0), (1, 1), (3, 0), (3, 1), (4, 1))
    after = {
        0: (((1, 0),), ()),
        1: (((4, 0),), ((2, 0),)),
        2: (((1, 1),), ((2, 1),)),
        3: (((3, 0),), ((1, 0),)),
        4: (((4, 1),), ((4, 0),)),
        5: (((3, 1),), ((1, 1),)),
        6: ((), ((3, 0),)),
        7: ((), ((3, 1),)),
    }

    arrived(2, 0)
    arrived(2, 1)

    def body(step, carry):
        m, c = jnp.int32(0), jnp.int32(0)
        for i, (far, part) in enumerate(order):
            here = (step == i).astype(jnp.int32)
            m += far * here
            c += part * here
        slot = lax.rem(m - 1 + odd, hops)
        to_sib(slot + odd, c).wait_recv()
        far_blocks(m, slot, c)
        part_to_sib(slot, c).start()

        for i, (fresh, done) in after.items():

            @pl.when(step == i)
            def _():
                for pair in done:
                    send_back_far(*pair)
                for pair in fresh:
                    arrived(*pair)

        return carry

    lax.fori_loop(0, len(order), body, 0)

    out_query_ref[...] = (acc[...] * factor).astype(BF16)
    send_back(4, 1)

    @pl.when(turn_mate)
    def _():
        send_back(2, 1)

    @pl.when(odd == 0)
    def _():
        for c in (0, 1):
            part_to_sib(0, c).wait_recv()
            own_part[:, parts[c]] += sib_part[0, c] * row_last[:, c * half : c * half + half]

    def add_back(m, c):
        @pl.when(returns(m, c))
        def _():
            ret(m, c).wait_recv()
            own_part[:, parts[c]] += (
                ret_in[m - 1, c].astype(F32) * row_last[:, c * half : c * half + half]
            )

    for m in (2, 1, 4):
        for c in (0, 1):
            add_back(m, c)
    for c in (0, 1):
        add_back(3, c)
        out_key_ref[parts[c]] = (own_part[pl.ds(0, dh), parts[c]] * factor).T.astype(BF16)
        out_value_ref[parts[c]] = own_part[pl.ds(dh, dh), parts[c]].T.astype(BF16)

    for c in (0, 1):
        for m in (1, 2):
            pl.when(sends(m, c))(fwd(m, c).wait_send)
            pl.when(relays(m))(relay(m, c).wait_send)
        if c == 0:
            pl.when(turn_mate)(cross(c).wait_send)
        if c == 1:
            pl.when(turn)(aside(c).wait_send)
            pl.when((me >= 2) & jnp.logical_not(turn))(ret(1, c).wait_send)
        else:
            pl.when(me >= 2)(ret(1, c).wait_send)
        for m in range(2, hops + 1):
            pl.when(me >= 2 * m)(ret(m, c).wait_send)
        for slot in range(hops):
            part_to_sib(slot, c).wait_send()
            to_sib(slot + odd, c).wait_send()


def hand_on(q_in, k_in, v_in, q_out, k_out, v_out, sem):
    size = q_in.shape[0] // 4
    pairs = [(q_in.at[pl.ds(i * size, size)], q_out.at[pl.ds(i * size, size)]) for i in range(4)]
    pairs += [(k_in, k_out), (v_in, v_out)]
    copies = [
        pltpu.make_async_copy(src, dst, sem.at[i]) for i, (src, dst) in enumerate(pairs)
    ]
    for copy in copies:
        copy.start()
    for copy in copies:
        copy.wait()


def solution(mesh):
    seq, fold = mesh.shape["seq"], mesh.shape["fold"]

    def body(query, keys, values, grad_out, head_bias, doc_ids):
        rows, dh = keys.shape
        heads = query.shape[1] // dh
        hops = MAXDOC // rows // 2
        wide = heads * dh
        block = rows + 16
        vmem = pl.BlockSpec(memory_space=pltpu.VMEM)
        hbm = pl.BlockSpec(memory_space=pl.ANY)
        dma = pltpu.SemaphoreType.DMA
        shapes = (
            jax.ShapeDtypeStruct((rows, wide), BF16),
            jax.ShapeDtypeStruct((rows, dh), BF16),
            jax.ShapeDtypeStruct((rows, dh), BF16),
        )
        grads = pl.pallas_call(
            functools.partial(kernel, seq, fold, rows, dh, heads),
            out_shape=tuple(pltpu.VMEM(x.shape, x.dtype) for x in shapes),
            in_specs=[hbm] * 6,
            out_specs=(vmem, vmem, vmem),
            scratch_shapes=[
                pltpu.VMEM((rows, wide), BF16),
                pltpu.VMEM((wide, rows), BF16),
                pltpu.VMEM((rows, wide), BF16),
                pltpu.VMEM((wide, rows), BF16),
                pltpu.VMEM((rows, wide), BF16),
                pltpu.VMEM((wide, rows), BF16),
                pltpu.VMEM((rows, dh), BF16),
                pltpu.VMEM((hops + 1, 2, block, dh), BF16),
                pltpu.VMEM((hops, 2, block, dh), BF16),
                pltpu.VMEM((rows, wide), F32),
                pltpu.VMEM((2 * dh, rows), F32),
                pltpu.VMEM((hops, 2, 2 * dh, rows // 2), F32),
                pltpu.VMEM((hops, 2, 2 * dh, rows // 2), F32),
                pltpu.VMEM((hops, 2, 2 * dh, rows // 2), F32),
                pltpu.VMEM((hops, 2, 2 * dh, rows // 2), BF16),
                pltpu.VMEM((hops, 2, 2 * dh, rows // 2), BF16),
                pltpu.VMEM((2, 2 * dh, rows // 2), BF16),
                pltpu.SMEM((heads,), F32),
                pltpu.VMEM((rows,), jnp.int32),
                dma((7,)),
                dma((2 * hops + 2,)), dma((2 * hops,)),
                dma((2 * hops,)), dma((2 * hops,)),
                dma((2 * hops,)), dma((2 * hops,)),
                dma((2 * hops,)), dma((2 * hops,)),
                dma((2,)), dma((2,)),
            ],
            compiler_params=pltpu.CompilerParams(
                collective_id=0, has_side_effects=True, vmem_limit_bytes=58 << 20
            ),
        )(head_bias, doc_ids, query, keys, values, grad_out)
        return pl.pallas_call(
            hand_on,
            out_shape=shapes,
            in_specs=[vmem] * 3,
            out_specs=(hbm,) * 3,
            scratch_shapes=[dma((6,))],
            compiler_params=pltpu.CompilerParams(vmem_limit_bytes=1 << 20),
        )(*grads)

    split = P(("seq", "fold"), None)
    return jax.shard_map(
        body,
        mesh=mesh,
        in_specs=(split, split, split, split, P(), P(("seq", "fold"))),
        out_specs=(split, split, split),
        check_vma=False,
    )
```

```python
import functools
import math

import jax
import jax.numpy as jnp
from jax import lax
from jax.experimental import pallas as pl
from jax.experimental.pallas import tpu as pltpu
from jax.sharding import PartitionSpec as P

MAXDOC = 2048
MESH = pl.DeviceIdType.MESH
LOG2E = math.log2(math.e)
F32 = jnp.float32
BF16 = jnp.bfloat16


def dot_nt(a, b):
    return lax.dot_general(a, b, (((1,), (1,)), ((), ())), preferred_element_type=F32)


def dot_nn(a, b):
    return jnp.dot(a, b, preferred_element_type=F32)


def kernel(
    seq, fold, rows, dh, heads,
    bias_hbm, ids_hbm, query_ref, keys_ref, values_ref, grad_ref,
    out_query_ref, out_key_ref, out_value_ref,
    q_nat, q_tra, do_nat, do_tra, dom_nat, dom_tra, v_own,
    blocks, sib_blocks, acc, own_part, part_d, part_o, sib_part, ret_out, ret_in, aside_in,
    bias_ref, ids_ref, load_sem, fwd_send, fwd_recv, sib_send, sib_recv, sibp_send, sibp_recv, ret_send, ret_recv,
    aside_send, aside_recv,
):
    peers = seq * fold
    me = lax.axis_index("seq") * fold + lax.axis_index("fold")
    odd = lax.rem(me, 2)
    hops = MAXDOC // rows // 2
    half = rows // 2
    factor = 1.0 / math.sqrt(dh)
    run = peers // 4

    def device(index):
        index = lax.rem(index + peers, peers)
        return (index // fold, lax.rem(index, fold))

    def turns(index):
        return (index >= run) & (index < peers) & (lax.rem(index, run) < 2)

    sibling = device(me + 1 - 2 * odd)
    turn = turns(me)
    turn_mate = turns(me - 2)
    turn_ahead = turns(me + 2)

    cols = [pl.ds(h * dh, dh) for h in range(heads)]
    parts = [pl.ds(c * half, half) for c in (0, 1)]
    k_rows, v_rows, id_rows = pl.ds(0, half), pl.ds(half, half), pl.ds(rows, 16)
    loads = [
        pltpu.make_async_copy(keys_ref.at[parts[0]], blocks.at[0, 0, k_rows], load_sem.at[0]),
        pltpu.make_async_copy(keys_ref.at[parts[1]], blocks.at[0, 1, k_rows], load_sem.at[1]),
        pltpu.make_async_copy(values_ref, v_own, load_sem.at[2]),
        pltpu.make_async_copy(ids_hbm, ids_ref, load_sem.at[3]),
        pltpu.make_async_copy(bias_hbm, bias_ref, load_sem.at[4]),
        pltpu.make_async_copy(query_ref, q_nat, load_sem.at[5]),
        pltpu.make_async_copy(grad_ref, do_nat, load_sem.at[6]),
    ]
    for load in loads:
        load.start()

    barrier = pltpu.get_barrier_semaphore()
    partners = jnp.int32(1)
    for hop in range(1, hops + 1):
        for far in (2 * hop, -2 * hop):
            valid = (me + far >= 0) & (me + far < peers)
            partners += valid.astype(jnp.int32)

            @pl.when(valid)
            def _():
                pl.semaphore_signal(
                    barrier, inc=1, device_id=device(me + far), device_id_type=MESH
                )

    pl.semaphore_signal(barrier, inc=1, device_id=sibling, device_id_type=MESH)

    loads[3].wait()

    ids_row = ids_ref[...].astype(F32).reshape(1, rows)
    first = ids_row[:, 0:1]
    last = ids_row[:, rows - 1 : rows]
    col_last = (jnp.broadcast_to(ids_row, (dh, rows)).T == last).astype(BF16)

    def push(src, dst, c, far, extra=0):
        slot = 2 * (dst - 1) + c
        return pltpu.make_async_remote_copy(
            blocks.at[src, c], blocks.at[dst, c],
            fwd_send.at[slot + extra], fwd_recv.at[slot],
            device_id=device(me + far), device_id_type=MESH,
        )

    def fwd(m, c):
        return push(0, m, c, 2 * m)

    def relay(m, c):
        return push(m, m + 2, c, 4)

    def cross(c):
        return push(2, 1, c, -2, 2 * hops)

    def sends(m, c):
        if m == 1 and c == 0:
            return (me + 2 < peers) & jnp.logical_not(turn_ahead)
        return me + 2 * m < peers

    def returns(m, c):
        if m == 1 and c == 1:
            return (me + 2 < peers) & jnp.logical_not(turn_ahead)
        return me + 2 * m < peers

    def relays(m):
        return (me >= 2 * m) & (me + 4 < peers)

    def to_sib(m, c):
        slot = m - odd
        return pltpu.make_async_remote_copy(
            blocks.at[m, c], sib_blocks.at[slot, c],
            sib_send.at[2 * slot + c], sib_recv.at[2 * slot + c],
            device_id=sibling, device_id_type=MESH,
        )

    def part_to_sib(slot, c):
        return pltpu.make_async_remote_copy(
            part_o.at[slot, c], sib_part.at[slot, c],
            sibp_send.at[2 * slot + c], sibp_recv.at[2 * slot + c],
            device_id=sibling, device_id_type=MESH,
        )

    def ret(m, c):
        slot = 2 * (m - 1) + c
        return pltpu.make_async_remote_copy(
            ret_out.at[m - 1, c], ret_in.at[m - 1, c], ret_send.at[slot], ret_recv.at[slot],
            device_id=device(me - 2 * m), device_id_type=MESH,
        )

    def aside(c):
        return pltpu.make_async_remote_copy(
            ret_out.at[0, c], aside_in.at[c], aside_send.at[c], aside_recv.at[c],
            device_id=device(me + 2), device_id_type=MESH,
        )

    for load in loads[:3]:
        load.wait()
    for c in (0, 1):
        blocks[0, c, v_rows] = v_own[parts[c]] * col_last[c * half : c * half + half]
        blocks[0, c, id_rows] = jnp.broadcast_to(last, (16, dh)).astype(BF16)
    pl.semaphore_wait(barrier, partners)
    for c in (0, 1):
        for m in (1, 2):
            pl.when(sends(m, c))(fwd(m, c).start)

    @pl.when(odd == 0)
    def _():
        for c in (0, 1):
            to_sib(0, c).start()

    ids_u = jnp.broadcast_to(ids_row, (rows, rows))
    ids_t = ids_u.T
    col_first = (ids_t[:, :dh] == first).astype(BF16)
    row_first = (ids_row == first).astype(BF16)
    row_last = (ids_row == last).astype(F32)
    for load in loads[4:]:
        load.wait()
    for h in range(heads):
        q_tra[cols[h], :] = q_nat[:, cols[h]].T
        do_tra[cols[h], :] = do_nat[:, cols[h]].T
    for h in range(heads):
        dom_nat[:, cols[h]] = do_nat[:, cols[h]] * col_first
        dom_tra[cols[h], :] = do_tra[cols[h], :] * row_first

    def block(k, v, g_nat, g_tra, mask):
        def scores(h):
            return dot_nt(q_nat[:, cols[h]], k), dot_nt(g_nat[:, cols[h]], v)

        grad_k = jnp.zeros((dh, rows), F32)
        grad_v = jnp.zeros((dh, rows), F32)
        ahead = scores(0)
        for h in range(heads):
            s, dp = ahead
            if h + 1 < heads:
                ahead = scores(h + 1)
            grow = jnp.exp2(s * (-factor * LOG2E) + bias_ref[h] * (-LOG2E))
            p = 1.0 / (1.0 + grow)
            if mask is not None:
                p = p * mask
            ds = (dp * (p * (1.0 - p))).astype(BF16)
            p = p.astype(BF16)
            if mask is not None:
                acc[:, cols[h]] = dot_nn(ds, k)
            else:
                acc[:, cols[h]] += dot_nn(ds, k)
            grad_v = grad_v + dot_nn(g_tra[cols[h], :], p)
            grad_k = grad_k + dot_nn(q_tra[cols[h], :], ds)
        return grad_k, grad_v

    iota_t = lax.broadcasted_iota(jnp.int32, (rows, rows), 0)
    iota_u = lax.broadcasted_iota(jnp.int32, (rows, rows), 1)
    own_mask = ((ids_t == ids_u) & (iota_u <= iota_t)).astype(F32)
    own_k = jnp.concatenate([blocks[0, c, k_rows] for c in (0, 1)], axis=0)
    grad_k, grad_v = block(own_k, v_own[...], do_nat, do_tra, own_mask)
    own_part[pl.ds(0, dh)] = grad_k
    own_part[pl.ds(dh, dh)] = grad_v

    def arrived(m, c):
        pl.when(me >= 2 * m)(fwd(m, c).wait_recv)

        @pl.when(me < 2 * m)
        def _():
            blocks[m, c] = jnp.full((rows + 16, dh), -1.0, BF16)

        if m <= 2:
            pl.when(relays(m))(relay(m, c).start)
        if m == 2 and c == 0:
            pl.when(turn_mate)(cross(c).start)
        pl.when(m - odd < hops)(to_sib(m, c).start)

    def far_blocks(m, slot, c):
        refs = (blocks.at[m, c], sib_blocks.at[slot, c])
        gates = [(ref[id_rows][0:1].astype(F32) == first).astype(F32) for ref in refs]
        k = jnp.concatenate([ref[k_rows] for ref in refs], axis=0)
        v = jnp.concatenate(
            [ref[v_rows] * gate.astype(BF16) for ref, gate in zip(refs, gates)], axis=0
        )
        grad_k, grad_v = block(k, v, dom_nat, dom_tra, None)
        grad_v = grad_v * jnp.concatenate(gates, axis=1)
        part_d[m - 1, c, pl.ds(0, dh)] = grad_k[:, :half]
        part_d[m - 1, c, pl.ds(dh, dh)] = grad_v[:, :half]
        part_o[slot, c, pl.ds(0, dh)] = grad_k[:, half:]
        part_o[slot, c, pl.ds(dh, dh)] = grad_v[:, half:]

    def send_back(m, c):
        back = m - odd

        @pl.when(back < hops)
        def _():
            part_to_sib(back, c).wait_recv()
            ret_out[m - 1, c] = (part_d[m - 1, c] + sib_part[back, c]).astype(BF16)

        @pl.when(back >= hops)
        def _():
            ret_out[m - 1, c] = part_d[m - 1, c].astype(BF16)

        if m == 2 and c == 1:

            @pl.when(turn_mate)
            def _():
                aside(c).wait_recv()
                ret_out[1, c] = (
                    ret_out[1, c].astype(F32) + aside_in[c].astype(F32)
                ).astype(BF16)

        if m == 1 and c == 1:
            pl.when(turn)(aside(c).start)
            pl.when((me >= 2) & jnp.logical_not(turn))(ret(m, c).start)
        else:
            pl.when(me >= 2 * m)(ret(m, c).start)

    def send_back_far(m, c):
        if m == 2 and c == 1:
            pl.when(jnp.logical_not(turn_mate))(functools.partial(send_back, m, c))
        else:
            send_back(m, c)

    order = ((2, 0), (2, 1), (1, 0), (4, 0), (1, 1), (3, 0), (3, 1), (4, 1))
    after = {
        0: (((1, 0),), ()),
        1: (((4, 0),), ((2, 0),)),
        2: (((1, 1),), ((2, 1),)),
        3: (((3, 0),), ((1, 0),)),
        4: (((4, 1),), ((4, 0),)),
        5: (((3, 1),), ((1, 1),)),
        6: ((), ((3, 0),)),
        7: ((), ((3, 1),)),
    }

    arrived(2, 0)
    arrived(2, 1)

    def body(step, carry):
        m, c = jnp.int32(0), jnp.int32(0)
        for i, (far, part) in enumerate(order):
            here = (step == i).astype(jnp.int32)
            m += far * here
            c += part * here
        slot = lax.rem(m - 1 + odd, hops)
        to_sib(slot + odd, c).wait_recv()
        far_blocks(m, slot, c)
        part_to_sib(slot, c).start()

        for i, (fresh, done) in after.items():

            @pl.when(step == i)
            def _():
                for pair in done:
                    send_back_far(*pair)
                for pair in fresh:
                    arrived(*pair)

        return carry

    lax.fori_loop(0, len(order), body, 0)

    out_query_ref[...] = (acc[...] * factor).astype(BF16)
    send_back(4, 1)

    @pl.when(turn_mate)
    def _():
        send_back(2, 1)

    @pl.when(odd == 0)
    def _():
        for c in (0, 1):
            part_to_sib(0, c).wait_recv()
            own_part[:, parts[c]] += sib_part[0, c] * row_last[:, c * half : c * half + half]

    def add_back(m, c):
        @pl.when(returns(m, c))
        def _():
            ret(m, c).wait_recv()
            own_part[:, parts[c]] += (
                ret_in[m - 1, c].astype(F32) * row_last[:, c * half : c * half + half]
            )

    for m in (2, 1, 4):
        for c in (0, 1):
            add_back(m, c)
    for c in (0, 1):
        add_back(3, c)
        out_key_ref[parts[c]] = (own_part[pl.ds(0, dh), parts[c]] * factor).T.astype(BF16)
        out_value_ref[parts[c]] = own_part[pl.ds(dh, dh), parts[c]].T.astype(BF16)

    for c in (0, 1):
        for m in (1, 2):
            pl.when(sends(m, c))(fwd(m, c).wait_send)
            pl.when(relays(m))(relay(m, c).wait_send)
        if c == 0:
            pl.when(turn_mate)(cross(c).wait_send)
        if c == 1:
            pl.when(turn)(aside(c).wait_send)
            pl.when((me >= 2) & jnp.logical_not(turn))(ret(1, c).wait_send)
        else:
            pl.when(me >= 2)(ret(1, c).wait_send)
        for m in range(2, hops + 1):
            pl.when(me >= 2 * m)(ret(m, c).wait_send)
        for slot in range(hops):
            part_to_sib(slot, c).wait_send()
            to_sib(slot + odd, c).wait_send()


def hand_on(q_in, k_in, v_in, q_out, k_out, v_out, sem):
    size = q_in.shape[0] // 4
    pairs = [(q_in.at[pl.ds(i * size, size)], q_out.at[pl.ds(i * size, size)]) for i in range(4)]
    pairs += [(k_in, k_out), (v_in, v_out)]
    copies = [
        pltpu.make_async_copy(src, dst, sem.at[i]) for i, (src, dst) in enumerate(pairs)
    ]
    for copy in copies:
        copy.start()
    for copy in copies:
        copy.wait()


def solution(mesh):
    seq, fold = mesh.shape["seq"], mesh.shape["fold"]

    def body(query, keys, values, grad_out, head_bias, doc_ids):
        rows, dh = keys.shape
        heads = query.shape[1] // dh
        hops = MAXDOC // rows // 2
        wide = heads * dh
        block = rows + 16
        vmem = pl.BlockSpec(memory_space=pltpu.VMEM)
        hbm = pl.BlockSpec(memory_space=pl.ANY)
        dma = pltpu.SemaphoreType.DMA
        shapes = (
            jax.ShapeDtypeStruct((rows, wide), BF16),
            jax.ShapeDtypeStruct((rows, dh), BF16),
            jax.ShapeDtypeStruct((rows, dh), BF16),
        )
        grads = pl.pallas_call(
            functools.partial(kernel, seq, fold, rows, dh, heads),
            out_shape=tuple(pltpu.VMEM(x.shape, x.dtype) for x in shapes),
            in_specs=[hbm] * 6,
            out_specs=(vmem, vmem, vmem),
            scratch_shapes=[
                pltpu.VMEM((rows, wide), BF16),
                pltpu.VMEM((wide, rows), BF16),
                pltpu.VMEM((rows, wide), BF16),
                pltpu.VMEM((wide, rows), BF16),
                pltpu.VMEM((rows, wide), BF16),
                pltpu.VMEM((wide, rows), BF16),
                pltpu.VMEM((rows, dh), BF16),
                pltpu.VMEM((hops + 1, 2, block, dh), BF16),
                pltpu.VMEM((hops, 2, block, dh), BF16),
                pltpu.VMEM((rows, wide), F32),
                pltpu.VMEM((2 * dh, rows), F32),
                pltpu.VMEM((hops, 2, 2 * dh, rows // 2), F32),
                pltpu.VMEM((hops, 2, 2 * dh, rows // 2), F32),
                pltpu.VMEM((hops, 2, 2 * dh, rows // 2), F32),
                pltpu.VMEM((hops, 2, 2 * dh, rows // 2), BF16),
                pltpu.VMEM((hops, 2, 2 * dh, rows // 2), BF16),
                pltpu.VMEM((2, 2 * dh, rows // 2), BF16),
                pltpu.SMEM((heads,), F32),
                pltpu.VMEM((rows,), jnp.int32),
                dma((7,)),
                dma((2 * hops + 2,)), dma((2 * hops,)),
                dma((2 * hops,)), dma((2 * hops,)),
                dma((2 * hops,)), dma((2 * hops,)),
                dma((2 * hops,)), dma((2 * hops,)),
                dma((2,)), dma((2,)),
            ],
            compiler_params=pltpu.CompilerParams(
                collective_id=0, has_side_effects=True, vmem_limit_bytes=58 << 20
            ),
        )(head_bias, doc_ids, query, keys, values, grad_out)
        return pl.pallas_call(
            hand_on,
            out_shape=shapes,
            in_specs=[vmem] * 3,
            out_specs=(hbm,) * 3,
            scratch_shapes=[dma((6,))],
            compiler_params=pltpu.CompilerParams(vmem_limit_bytes=1 << 20),
        )(*grads)

    split = P(("seq", "fold"), None)
    return jax.shard_map(
        body,
        mesh=mesh,
        in_specs=(split, split, split, split, P(), P(("seq", "fold"))),
        out_specs=(split, split, split),
        check_vma=False,
    )
```

```python
import functools
import math

import jax
import jax.numpy as jnp
from jax import lax
from jax.experimental import pallas as pl
from jax.experimental.pallas import tpu as pltpu
from jax.sharding import PartitionSpec as P

MAXDOC = 2048
MESH = pl.DeviceIdType.MESH
LOG2E = math.log2(math.e)
F32 = jnp.float32
BF16 = jnp.bfloat16


def dot_nt(a, b):
    return lax.dot_general(a, b, (((1,), (1,)), ((), ())), preferred_element_type=F32)


def dot_nn(a, b):
    return jnp.dot(a, b, preferred_element_type=F32)


def kernel(
    seq, fold, rows, dh, heads,
    bias_hbm, ids_hbm, query_ref, keys_ref, values_ref, grad_ref,
    out_query_ref, out_key_ref, out_value_ref,
    q_nat, q_tra, do_nat, do_tra, dom_nat, dom_tra, v_own,
    blocks, sib_blocks, acc, own_part, part_d, part_o, sib_part, ret_out, ret_in, aside_in,
    bias_ref, ids_ref, load_sem, fwd_send, fwd_recv, sib_send, sib_recv, sibp_send, sibp_recv, ret_send, ret_recv,
    aside_send, aside_recv,
):
    peers = seq * fold
    me = lax.axis_index("seq") * fold + lax.axis_index("fold")
    odd = lax.rem(me, 2)
    hops = MAXDOC // rows // 2
    half = rows // 2
    factor = 1.0 / math.sqrt(dh)
    run = peers // 4

    def device(index):
        index = lax.rem(index + peers, peers)
        return (index // fold, lax.rem(index, fold))

    def turns(index):
        return (index >= run) & (index < peers) & (lax.rem(index, run) < 2)

    sibling = device(me + 1 - 2 * odd)
    turn = turns(me)
    turn_mate = turns(me - 2)
    turn_ahead = turns(me + 2)

    cols = [pl.ds(h * dh, dh) for h in range(heads)]
    parts = [pl.ds(c * half, half) for c in (0, 1)]
    k_rows, v_rows, id_rows = pl.ds(0, half), pl.ds(half, half), pl.ds(rows, 16)
    loads = [
        pltpu.make_async_copy(keys_ref.at[parts[0]], blocks.at[0, 0, k_rows], load_sem.at[0]),
        pltpu.make_async_copy(keys_ref.at[parts[1]], blocks.at[0, 1, k_rows], load_sem.at[1]),
        pltpu.make_async_copy(values_ref, v_own, load_sem.at[2]),
        pltpu.make_async_copy(ids_hbm, ids_ref, load_sem.at[3]),
        pltpu.make_async_copy(bias_hbm, bias_ref, load_sem.at[4]),
        pltpu.make_async_copy(query_ref, q_nat, load_sem.at[5]),
        pltpu.make_async_copy(grad_ref, do_nat, load_sem.at[6]),
    ]
    for load in loads:
        load.start()

    barrier = pltpu.get_barrier_semaphore()
    partners = jnp.int32(1)
    for hop in range(1, hops + 1):
        for far in (2 * hop, -2 * hop):
            valid = (me + far >= 0) & (me + far < peers)
            partners += valid.astype(jnp.int32)

            @pl.when(valid)
            def _():
                pl.semaphore_signal(
                    barrier, inc=1, device_id=device(me + far), device_id_type=MESH
                )

    pl.semaphore_signal(barrier, inc=1, device_id=sibling, device_id_type=MESH)

    loads[3].wait()

    ids_row = ids_ref[...].astype(F32).reshape(1, rows)
    first = ids_row[:, 0:1]
    last = ids_row[:, rows - 1 : rows]
    col_last = (jnp.broadcast_to(ids_row, (dh, rows)).T == last).astype(BF16)

    def push(src, dst, c, far, extra=0):
        slot = 2 * (dst - 1) + c
        return pltpu.make_async_remote_copy(
            blocks.at[src, c], blocks.at[dst, c],
            fwd_send.at[slot + extra], fwd_recv.at[slot],
            device_id=device(me + far), device_id_type=MESH,
        )

    def fwd(m, c):
        return push(0, m, c, 2 * m)

    def relay(m, c):
        return push(m, m + 2, c, 4)

    def cross(c):
        return push(2, 1, c, -2, 2 * hops)

    def sends(m, c):
        if m == 1 and c == 0:
            return (me + 2 < peers) & jnp.logical_not(turn_ahead)
        return me + 2 * m < peers

    def returns(m, c):
        if m == 1 and c == 1:
            return (me + 2 < peers) & jnp.logical_not(turn_ahead)
        return me + 2 * m < peers

    def relays(m):
        return (me >= 2 * m) & (me + 4 < peers)

    def to_sib(m, c):
        slot = m - odd
        return pltpu.make_async_remote_copy(
            blocks.at[m, c], sib_blocks.at[slot, c],
            sib_send.at[2 * slot + c], sib_recv.at[2 * slot + c],
            device_id=sibling, device_id_type=MESH,
        )

    def part_to_sib(slot, c):
        return pltpu.make_async_remote_copy(
            part_o.at[slot, c], sib_part.at[slot, c],
            sibp_send.at[2 * slot + c], sibp_recv.at[2 * slot + c],
            device_id=sibling, device_id_type=MESH,
        )

    def ret(m, c):
        slot = 2 * (m - 1) + c
        return pltpu.make_async_remote_copy(
            ret_out.at[m - 1, c], ret_in.at[m - 1, c], ret_send.at[slot], ret_recv.at[slot],
            device_id=device(me - 2 * m), device_id_type=MESH,
        )

    def aside(c):
        return pltpu.make_async_remote_copy(
            ret_out.at[0, c], aside_in.at[c], aside_send.at[c], aside_recv.at[c],
            device_id=device(me + 2), device_id_type=MESH,
        )

    for load in loads[:3]:
        load.wait()
    for c in (0, 1):
        blocks[0, c, v_rows] = v_own[parts[c]] * col_last[c * half : c * half + half]
        blocks[0, c, id_rows] = jnp.broadcast_to(last, (16, dh)).astype(BF16)
    pl.semaphore_wait(barrier, partners)
    for c in (0, 1):
        for m in (1, 2):
            pl.when(sends(m, c))(fwd(m, c).start)

    @pl.when(odd == 0)
    def _():
        for c in (0, 1):
            to_sib(0, c).start()

    ids_u = jnp.broadcast_to(ids_row, (rows, rows))
    ids_t = ids_u.T
    col_first = (ids_t[:, :dh] == first).astype(BF16)
    row_first = (ids_row == first).astype(BF16)
    row_last = (ids_row == last).astype(F32)
    for load in loads[4:]:
        load.wait()
    for h in range(heads):
        q_tra[cols[h], :] = q_nat[:, cols[h]].T
        do_tra[cols[h], :] = do_nat[:, cols[h]].T
    for h in range(heads):
        dom_nat[:, cols[h]] = do_nat[:, cols[h]] * col_first
        dom_tra[cols[h], :] = do_tra[cols[h], :] * row_first

    def block(k, v, g_nat, g_tra, mask):
        def scores(h):
            return dot_nt(q_nat[:, cols[h]], k), dot_nt(g_nat[:, cols[h]], v)

        grad_k = jnp.zeros((dh, rows), F32)
        grad_v = jnp.zeros((dh, rows), F32)
        ahead = scores(0)
        for h in range(heads):
            s, dp = ahead
            if h + 1 < heads:
                ahead = scores(h + 1)
            grow = jnp.exp2(s * (-factor * LOG2E) + bias_ref[h] * (-LOG2E))
            p = 1.0 / (1.0 + grow)
            if mask is not None:
                p = p * mask
            ds = (dp * (p * (1.0 - p))).astype(BF16)
            p = p.astype(BF16)
            if mask is not None:
                acc[:, cols[h]] = dot_nn(ds, k)
            else:
                acc[:, cols[h]] += dot_nn(ds, k)
            grad_v = grad_v + dot_nn(g_tra[cols[h], :], p)
            grad_k = grad_k + dot_nn(q_tra[cols[h], :], ds)
        return grad_k, grad_v

    iota_t = lax.broadcasted_iota(jnp.int32, (rows, rows), 0)
    iota_u = lax.broadcasted_iota(jnp.int32, (rows, rows), 1)
    own_mask = ((ids_t == ids_u) & (iota_u <= iota_t)).astype(F32)
    own_k = jnp.concatenate([blocks[0, c, k_rows] for c in (0, 1)], axis=0)
    grad_k, grad_v = block(own_k, v_own[...], do_nat, do_tra, own_mask)
    own_part[pl.ds(0, dh)] = grad_k
    own_part[pl.ds(dh, dh)] = grad_v

    def arrived(m, c):
        pl.when(me >= 2 * m)(fwd(m, c).wait_recv)

        @pl.when(me < 2 * m)
        def _():
            blocks[m, c] = jnp.full((rows + 16, dh), -1.0, BF16)

        if m <= 2:
            pl.when(relays(m))(relay(m, c).start)
        if m == 2 and c == 0:
            pl.when(turn_mate)(cross(c).start)
        pl.when(m - odd < hops)(to_sib(m, c).start)

    def far_blocks(m, slot, c):
        refs = (blocks.at[m, c], sib_blocks.at[slot, c])
        gates = [(ref[id_rows][0:1].astype(F32) == first).astype(F32) for ref in refs]
        k = jnp.concatenate([ref[k_rows] for ref in refs], axis=0)
        v = jnp.concatenate(
            [ref[v_rows] * gate.astype(BF16) for ref, gate in zip(refs, gates)], axis=0
        )
        grad_k, grad_v = block(k, v, dom_nat, dom_tra, None)
        grad_v = grad_v * jnp.concatenate(gates, axis=1)
        part_d[m - 1, c, pl.ds(0, dh)] = grad_k[:, :half]
        part_d[m - 1, c, pl.ds(dh, dh)] = grad_v[:, :half]
        part_o[slot, c, pl.ds(0, dh)] = grad_k[:, half:]
        part_o[slot, c, pl.ds(dh, dh)] = grad_v[:, half:]

    def send_back(m, c):
        back = m - odd

        @pl.when(back < hops)
        def _():
            part_to_sib(back, c).wait_recv()
            ret_out[m - 1, c] = (part_d[m - 1, c] + sib_part[back, c]).astype(BF16)

        @pl.when(back >= hops)
        def _():
            ret_out[m - 1, c] = part_d[m - 1, c].astype(BF16)

        if m == 2 and c == 1:

            @pl.when(turn_mate)
            def _():
                aside(c).wait_recv()
                ret_out[1, c] = (
                    ret_out[1, c].astype(F32) + aside_in[c].astype(F32)
                ).astype(BF16)

        if m == 1 and c == 1:
            pl.when(turn)(aside(c).start)
            pl.when((me >= 2) & jnp.logical_not(turn))(ret(m, c).start)
        else:
            pl.when(me >= 2 * m)(ret(m, c).start)

    def send_back_far(m, c):
        if m == 2 and c == 1:
            pl.when(jnp.logical_not(turn_mate))(functools.partial(send_back, m, c))
        else:
            send_back(m, c)

    order = ((2, 0), (2, 1), (1, 0), (4, 0), (1, 1), (3, 0), (3, 1), (4, 1))
    after = {
        0: (((1, 0),), ()),
        1: (((4, 0),), ((2, 0),)),
        2: (((1, 1),), ((2, 1),)),
        3: (((3, 0),), ((1, 0),)),
        4: (((4, 1),), ((4, 0),)),
        5: (((3, 1),), ((1, 1),)),
        6: ((), ((3, 0),)),
        7: ((), ((3, 1),)),
    }

    arrived(2, 0)
    arrived(2, 1)

    def body(step, carry):
        m, c = jnp.int32(0), jnp.int32(0)
        for i, (far, part) in enumerate(order):
            here = (step == i).astype(jnp.int32)
            m += far * here
            c += part * here
        slot = lax.rem(m - 1 + odd, hops)
        to_sib(slot + odd, c).wait_recv()
        far_blocks(m, slot, c)
        part_to_sib(slot, c).start()

        for i, (fresh, done) in after.items():

            @pl.when(step == i)
            def _():
                for pair in done:
                    send_back_far(*pair)
                for pair in fresh:
                    arrived(*pair)

        return carry

    lax.fori_loop(0, len(order), body, 0)

    out_query_ref[...] = (acc[...] * factor).astype(BF16)
    send_back(4, 1)

    @pl.when(turn_mate)
    def _():
        send_back(2, 1)

    @pl.when(odd == 0)
    def _():
        for c in (0, 1):
            part_to_sib(0, c).wait_recv()
            own_part[:, parts[c]] += sib_part[0, c] * row_last[:, c * half : c * half + half]

    def add_back(m, c):
        @pl.when(returns(m, c))
        def _():
            ret(m, c).wait_recv()
            own_part[:, parts[c]] += (
                ret_in[m - 1, c].astype(F32) * row_last[:, c * half : c * half + half]
            )

    for m in (2, 1, 4):
        for c in (0, 1):
            add_back(m, c)
    for c in (0, 1):
        add_back(3, c)
        out_key_ref[parts[c]] = (own_part[pl.ds(0, dh), parts[c]] * factor).T.astype(BF16)
        out_value_ref[parts[c]] = own_part[pl.ds(dh, dh), parts[c]].T.astype(BF16)

    for c in (0, 1):
        for m in (1, 2):
            pl.when(sends(m, c))(fwd(m, c).wait_send)
            pl.when(relays(m))(relay(m, c).wait_send)
        if c == 0:
            pl.when(turn_mate)(cross(c).wait_send)
        if c == 1:
            pl.when(turn)(aside(c).wait_send)
            pl.when((me >= 2) & jnp.logical_not(turn))(ret(1, c).wait_send)
        else:
            pl.when(me >= 2)(ret(1, c).wait_send)
        for m in range(2, hops + 1):
            pl.when(me >= 2 * m)(ret(m, c).wait_send)
        for slot in range(hops):
            part_to_sib(slot, c).wait_send()
            to_sib(slot + odd, c).wait_send()


def hand_on(q_in, k_in, v_in, q_out, k_out, v_out, sem):
    size = q_in.shape[0] // 8
    pairs = [(q_in.at[pl.ds(i * size, size)], q_out.at[pl.ds(i * size, size)]) for i in range(8)]
    pairs += [(k_in, k_out), (v_in, v_out)]
    copies = [
        pltpu.make_async_copy(src, dst, sem.at[i]) for i, (src, dst) in enumerate(pairs)
    ]
    for copy in copies:
        copy.start()
    for copy in copies:
        copy.wait()


def solution(mesh):
    seq, fold = mesh.shape["seq"], mesh.shape["fold"]

    def body(query, keys, values, grad_out, head_bias, doc_ids):
        rows, dh = keys.shape
        heads = query.shape[1] // dh
        hops = MAXDOC // rows // 2
        wide = heads * dh
        block = rows + 16
        vmem = pl.BlockSpec(memory_space=pltpu.VMEM)
        hbm = pl.BlockSpec(memory_space=pl.ANY)
        dma = pltpu.SemaphoreType.DMA
        shapes = (
            jax.ShapeDtypeStruct((rows, wide), BF16),
            jax.ShapeDtypeStruct((rows, dh), BF16),
            jax.ShapeDtypeStruct((rows, dh), BF16),
        )
        grads = pl.pallas_call(
            functools.partial(kernel, seq, fold, rows, dh, heads),
            out_shape=tuple(pltpu.VMEM(x.shape, x.dtype) for x in shapes),
            in_specs=[hbm] * 6,
            out_specs=(vmem, vmem, vmem),
            scratch_shapes=[
                pltpu.VMEM((rows, wide), BF16),
                pltpu.VMEM((wide, rows), BF16),
                pltpu.VMEM((rows, wide), BF16),
                pltpu.VMEM((wide, rows), BF16),
                pltpu.VMEM((rows, wide), BF16),
                pltpu.VMEM((wide, rows), BF16),
                pltpu.VMEM((rows, dh), BF16),
                pltpu.VMEM((hops + 1, 2, block, dh), BF16),
                pltpu.VMEM((hops, 2, block, dh), BF16),
                pltpu.VMEM((rows, wide), F32),
                pltpu.VMEM((2 * dh, rows), F32),
                pltpu.VMEM((hops, 2, 2 * dh, rows // 2), F32),
                pltpu.VMEM((hops, 2, 2 * dh, rows // 2), F32),
                pltpu.VMEM((hops, 2, 2 * dh, rows // 2), F32),
                pltpu.VMEM((hops, 2, 2 * dh, rows // 2), BF16),
                pltpu.VMEM((hops, 2, 2 * dh, rows // 2), BF16),
                pltpu.VMEM((2, 2 * dh, rows // 2), BF16),
                pltpu.SMEM((heads,), F32),
                pltpu.VMEM((rows,), jnp.int32),
                dma((7,)),
                dma((2 * hops + 2,)), dma((2 * hops,)),
                dma((2 * hops,)), dma((2 * hops,)),
                dma((2 * hops,)), dma((2 * hops,)),
                dma((2 * hops,)), dma((2 * hops,)),
                dma((2,)), dma((2,)),
            ],
            compiler_params=pltpu.CompilerParams(
                collective_id=0, has_side_effects=True, vmem_limit_bytes=58 << 20
            ),
        )(head_bias, doc_ids, query, keys, values, grad_out)
        return pl.pallas_call(
            hand_on,
            out_shape=shapes,
            in_specs=[vmem] * 3,
            out_specs=(hbm,) * 3,
            scratch_shapes=[dma((10,))],
            compiler_params=pltpu.CompilerParams(vmem_limit_bytes=1 << 20),
        )(*grads)

    split = P(("seq", "fold"), None)
    return jax.shard_map(
        body,
        mesh=mesh,
        in_specs=(split, split, split, split, P(), P(("seq", "fold"))),
        out_specs=(split, split, split),
        check_vma=False,
    )
```
